256 devices in a mesh: row: 8 (over z_hi, x), col: 32 (over z_lo, y, core).
Axes of the slice: x: 4, y: 4, z: 8 (z_hi: 2, z_lo: 4; z = z_hi * 4 + z_lo), core: 2. Of those that a mesh axis runs over, the one named last changes fastest.
Arguments:
- node_features: bfloat16 [32768, 512], P(('row', 'col')), may hold values from -6 to 6
- out_grad: bfloat16 [32768, 512], P(('row', 'col')), may hold values from -6 to 6
- adjacency: bfloat16 [32768, 32768], P('row', 'col'), may hold values from 0 to 1.5, as said below
- tile_mask: int32 [256, 256], P('row', 'col'), may hold values from 0 to 1, as said below
- degrees: int32 [32768], P(('row', 'col')), may hold values from 4 to 15
- w_self: bfloat16 [512, 512], replicated, may hold values from -0.25 to 0.25
- w_neigh: bfloat16 [512, 512], replicated, may hold values from -0.25 to 0.25
Outputs:
- in_grad: bfloat16 [32768, 512], P(('row', 'col'))
- grad_self: float32 [512, 512], replicated
- grad_neigh: float32 [512, 512], replicated
The draws below stay inside these ranges and needn't reach their ends.
Inputs may be any that keep to these rules, and one draw needn't show every extreme that they name: `adjacency`: zero where there is no edge; about one entry in 32 inside a tile is an edge. `tile_mask`: the share of tiles with edges differs between the blocks of 32 x 8 tiles.
All inputs are finite; a program needn't handle non-finite values.
Results may differ from the reference program's by a relative error of at most 0.0053.
Values may be sent and summed in bfloat16 or wider, within the bound.
A program may use at most 64 MiB of HBM per device.

```python
import jax
import jax.numpy as jnp
from jax import lax

F = 512
NODE_DEV = 128
NODES = 32768
TILES = 256
TILE_ROWS = 32
TILE_COLS = 8
N_ROW = 8
N_COL = 32


def draw_adjacency(key, part):
    key = jax.random.fold_in(key, 11)
    unit = jax.random.uniform(key, (NODES, NODES), jnp.float32)
    return jnp.where(unit < 1.0 / 32.0, 0.5 + 32.0 * unit, 0.0).astype(jnp.bfloat16)


def draw_tile_mask(key, part):
    key = jax.random.fold_in(key, 23)
    level_key, cell_key = jax.random.split(key)
    cell_rows = TILES // TILE_ROWS
    cell_cols = TILES // TILE_COLS
    levels = jax.random.randint(level_key, (cell_rows, cell_cols), 1, 9)
    levels = jnp.repeat(jnp.repeat(levels, TILE_ROWS, 0), TILE_COLS, 1)
    picks = jax.random.randint(cell_key, (TILES, TILES), 0, 8)
    return (picks < levels).astype(jnp.int32)


def plant(entries, own_key, low, top_value):
    dims = entries.shape
    spot = [jax.random.randint(jax.random.fold_in(own_key, axis), (), 0, dims[axis]) for axis in range(len(dims))]
    entries = entries.at[tuple(spot)].set(low)
    longest = dims.index(max(dims))
    spot[longest] = (spot[longest] + 1) % dims[longest]
    return entries.at[tuple(spot)].set(top_value)


def steps_of(rng, dims, cuts, low, top_value):
    factor_of, own = 1.0, jax.random.fold_in(rng, 6)
    for axis_at, shards_of in cuts:
        heights = jnp.exp(jax.random.uniform(jax.random.fold_in(own, axis_at), (shards_of,), jnp.float32, low / len(cuts), top_value / len(cuts)))
        factor_of = factor_of * jnp.repeat(heights, dims[axis_at] // shards_of).reshape([-1 if axis == axis_at else 1 for axis in range(len(dims))])
    return factor_of


def scatter_about(stream_key, dims, width, limit, cuts=(), kind=jnp.bfloat16):
    values = jax.random.normal(stream_key, dims, jnp.float32) * width
    if len(cuts) > 0:
        values = steps_of(stream_key, dims, cuts, -0.22, 0.18) * values
    return jnp.clip(values, min=-limit, max=limit).astype(kind)


def setup_inputs(seed: int = 0) -> dict:
    key_list = jax.random.split(jax.random.key(seed), 8)
    return {
        "node_features": scatter_about(key_list[0], (NODES, F), 1.0, 6.0, ((0, 256),)),
        "out_grad": scatter_about(key_list[1], (NODES, F), 1.0, 6.0, ((0, 256),)),
        "adjacency": draw_adjacency(jax.random.fold_in(key_list[7], 71), 0),
        "tile_mask": draw_tile_mask(jax.random.fold_in(key_list[7], 71), 0),
        "degrees": plant(jax.random.randint(key_list[4], (NODES,), 4, 16), jax.random.fold_in(key_list[4], 1), 4, 15).astype(jnp.int32),
        "w_self": scatter_about(key_list[5], (F, F), F ** -0.5, 0.25),
        "w_neigh": scatter_about(key_list[6], (F, F), F ** -0.5, 0.25),
    }


def reference(node_features, out_grad, adjacency, tile_mask, degrees, w_self, w_neigh):
    node_count, feat_width = node_features.shape
    blocks = tile_mask.shape[0]
    tile_size = node_count // blocks
    scaled = (out_grad.astype(jnp.float32) / degrees.astype(jnp.float32)[:, None]).astype(jnp.bfloat16)

    def row_block(running, inputs):
        adj_rows, mask_row, grad_rows = inputs
        col_mask = jnp.repeat(mask_row.astype(jnp.bfloat16), tile_size)
        edge_rows = adj_rows * col_mask[None, :]
        update = lax.dot_general(edge_rows, grad_rows, (((0,), (0,)), ((), ())), preferred_element_type=jnp.float32)
        return running + update, None

    start_value = jnp.zeros((node_count, feat_width), jnp.float32)
    pulled_cols, _ = lax.scan(row_block, start_value, (adjacency.reshape(blocks, tile_size, node_count), tile_mask, scaled.reshape(blocks, tile_size, feat_width)))
    pulled = pulled_cols.reshape(N_COL, N_ROW, NODE_DEV, feat_width).transpose(1, 0, 2, 3).reshape(node_count, feat_width)
    factor = float(node_count) ** -0.5
    grad_self = jnp.dot(node_features.T, out_grad, preferred_element_type=jnp.float32) * factor
    grad_neigh = jnp.dot(node_features.astype(jnp.float32).T, pulled, precision=lax.Precision.HIGHEST) * factor
    pulled_half = pulled.astype(jnp.bfloat16)
    own_term = lax.dot_general(out_grad, w_self, (((1,), (1,)), ((), ())), preferred_element_type=jnp.float32)
    neigh_term = lax.dot_general(pulled_half, w_neigh, (((1,), (1,)), ((), ())), preferred_element_type=jnp.float32)
    in_grad = (own_term + neigh_term).astype(jnp.bfloat16)
    return in_grad, grad_self, grad_neigh
```

```python
import math

import jax
import jax.numpy as jnp
from jax import lax
from jax.experimental import pallas as pl
from jax.experimental.pallas import tpu as pltpu
from jax.sharding import PartitionSpec as P

MESH = pl.DeviceIdType.MESH
F32, BF16 = jnp.float32, jnp.bfloat16
FEAT = 512
NODE = 128
PARTS = 2
CHUNK = FEAT // PARTS


def rdma(src, dst, send_sem, recv_sem, to):
    return pltpu.make_async_remote_copy(
        src_ref=src, dst_ref=dst, send_sem=send_sem, recv_sem=recv_sem, device_id=to, device_id_type=MESH
    )


class Place:
    def __init__(self):
        row, col = lax.axis_index("row"), lax.axis_index("col")
        self.row, self.col = row, col
        self.x, self.zh = lax.rem(row, 4), lax.div(row, 4)
        self.zl, self.y, self.k = lax.div(col, 8), lax.rem(lax.div(col, 2), 4), lax.rem(col, 2)
        self.z = self.zh * 4 + self.zl
        self.q = self.x * 4 + self.y

    def at(self, x=None, y=None, z=None, k=None):
        x = self.x if x is None else x
        y = self.y if y is None else y
        z = self.z if z is None else z
        k = self.k if k is None else k
        return (lax.div(z, 4) * 4 + x, lax.rem(z, 4) * 8 + y * 2 + k)

    def chip(self, d):
        q = lax.rem(self.q + d, 16)
        return q, self.at(x=lax.div(q, 4), y=lax.rem(q, 4))

    def along_z(self, d):
        z = lax.rem(self.z + d, 8)
        return z, self.at(z=z)

    def wait_recv(self, ref, sem):
        rdma(ref, ref, sem, sem, self.at()).wait_recv()

    def wait_send(self, ref, sem):
        rdma(ref, ref, sem, sem, self.at()).wait_send()


class Total:
    def __init__(self, place, rows, refs):
        self.place, self.rows, self.lanes, self.across = place, rows, rows, FEAT // rows
        self.part, self.kin, self.out_piece, self.in_piece, self.zbuf, self.whole, self.ss, self.rs = refs

    @staticmethod
    def scratch(rows):
        half = rows // 2
        return [
            pltpu.VMEM((2, half, FEAT), BF16),
            pltpu.VMEM((half, FEAT), BF16),
            pltpu.VMEM((16, 16, rows), BF16),
            pltpu.VMEM((16, 16, rows), BF16),
            pltpu.VMEM((8, 16, rows), BF16),
            pltpu.VMEM((2, 16, 16, rows), BF16),
            pltpu.SemaphoreType.DMA((5,)),
            pltpu.SemaphoreType.DMA((5,)),
        ]

    def spot(self, p):
        return slice((p // self.across) * 16, (p // self.across) * 16 + 16), slice(
            (p % self.across) * self.lanes, (p % self.across + 1) * self.lanes
        )

    def start(self, value):
        pc, half = self.place, self.rows // 2
        self.part[0] = value[:half].astype(BF16)
        self.part[1] = value[half:].astype(BF16)
        rdma(self.part.at[1 - pc.k], self.kin, self.ss.at[0], self.rs.at[0], pc.at(k=1 - pc.k)).start()

    def plane(self):
        pc = self.place
        pc.wait_recv(self.kin, self.rs.at[0])
        both = (self.part[pc.k].astype(F32) + self.kin[...].astype(F32)).astype(BF16)
        for p in range(16):
            self.out_piece[p] = both[self.spot(p)]

        def send(d, _):
            q, to = pc.chip(d)
            rdma(self.out_piece.at[q], self.in_piece.at[pc.q], self.ss.at[1], self.rs.at[1], to).start()
            return _

        lax.fori_loop(1, 16, send, 0)
        self.in_piece[pc.q] = self.out_piece[pc.q]

    def column(self):
        pc = self.place
        pc.wait_recv(self.in_piece.at[pl.ds(0, 15)], self.rs.at[1])
        self.zbuf[pc.z] = jnp.sum(self.in_piece[...].astype(F32), axis=0).astype(BF16)

        def send(d, _):
            z, to = pc.along_z(d)
            rdma(self.zbuf.at[pc.z], self.zbuf.at[pc.z], self.ss.at[2], self.rs.at[2], to).start()
            return _

        lax.fori_loop(1, 8, send, 0)

    def spread(self, factor):
        pc = self.place
        pc.wait_recv(self.zbuf.at[pl.ds(0, 7)], self.rs.at[2])
        self.whole[pc.k, pc.q] = (jnp.sum(self.zbuf[...].astype(F32), axis=0) * factor).astype(BF16)
        mine = self.whole.at[pc.k, pc.q]

        def send(d, _):
            q, to = pc.chip(d)
            rdma(mine, mine, self.ss.at[3], self.rs.at[3], to).start()
            return _

        lax.fori_loop(1, 16, send, 0)

    def cross(self):
        pc = self.place
        pc.wait_recv(self.whole.at[0, pl.ds(0, 15)], self.rs.at[3])
        mine = self.whole.at[pc.k]
        rdma(mine, mine, self.ss.at[4], self.rs.at[4], pc.at(k=1 - pc.k)).start()

    def finish(self, out_ref, base):
        pc, half = self.place, self.rows // 2
        pc.wait_recv(self.whole.at[0], self.rs.at[4])
        for h in range(2):
            for p in range(16):
                rows, lanes = self.spot(p)
                out_ref[base + h * half + rows.start : base + h * half + rows.stop, lanes] = self.whole[h, p]

    def drain(self):
        pc = self.place
        pc.wait_send(self.kin, self.ss.at[0])
        pc.wait_send(self.in_piece.at[pl.ds(0, 15)], self.ss.at[1])
        pc.wait_send(self.zbuf.at[pl.ds(0, 7)], self.ss.at[2])
        pc.wait_send(self.whole.at[0, pl.ds(0, 15)], self.ss.at[3])
        pc.wait_send(self.whole.at[0], self.ss.at[4])


def kernel(factor, *refs):
    nf_ref, og_ref, mask_ref, deg_ref, adj_ref, ws_hbm, wn_hbm = refs[:7]
    ig_ref, gs_ref, gn_ref = refs[7:10]
    (
        adj, wide_mask, gath, lhs, acc, part, rx, zout, zin, own, feats, ws, wn, grad_t, ig_t,
        local_sem, z_ss, z_rs, y_ss, y_rs, k_ss, k_rs, f_ss, f_rs, b_ss, b_rs,
    ) = refs[10:36]
    rest = refs[36:]
    pc = Place()
    sums = [Total(pc, rows, rest[8 * i : 8 * i + 8]) for i, rows in enumerate([FEAT] + [CHUNK] * PARTS)]
    all_self, all_neigh = sums[0], sums[1:]

    barrier = pltpu.get_barrier_semaphore()

    def hello(to):
        pl.semaphore_signal(barrier, inc=1, device_id=to, device_id_type=MESH)

    def hello_z(d, _):
        hello(pc.along_z(d)[1])
        return _

    def hello_plane(d, _):
        hello(pc.chip(d)[1])
        return _

    lax.fori_loop(1, 8, hello_z, 0)
    lax.fori_loop(1, 16, hello_plane, 0)
    hello(pc.at(k=1 - pc.k))

    def group(s):
        return jnp.bitwise_xor(pc.zl, s)

    def adj_copy(s):
        rows = pl.ds(pl.multiple_of(group(s) * 1024, 1024), 1024)
        return pltpu.make_async_copy(adj_ref.at[rows], adj.at[rows], local_sem.at[s])

    w_copies = [pltpu.make_async_copy(ws_hbm, ws, local_sem.at[4]), pltpu.make_async_copy(wn_hbm, wn, local_sem.at[5])]
    for s in range(4):
        adj_copy(s).start()
    for copy in w_copies:
        copy.start()

    turned = og_ref[...].astype(F32).T
    grad_t[...] = turned.astype(BF16)
    scaled_t = (turned / deg_ref[...].astype(F32)).astype(BF16)
    for ch in range(PARTS):
        gath[ch, pc.zl, pc.k, pc.y] = scaled_t[ch * CHUNK : (ch + 1) * CHUNK]
    feats[pc.row] = nf_ref[...]
    lane_tile = lax.div(lax.broadcasted_iota(jnp.int32, (8, 1024), 1), 128)
    pick = (lane_tile == lax.broadcasted_iota(jnp.int32, (8, 1024), 0)).astype(F32).astype(BF16)
    wide_mask[...] = jnp.dot(mask_ref[...].astype(F32).astype(BF16), pick, preferred_element_type=F32)

    pl.semaphore_wait(barrier, 23)

    for ch in range(PARTS):
        mine = gath.at[ch, pc.zl, pc.k, pc.y]
        for s in range(1, 4):
            rdma(mine, mine, z_ss, z_rs.at[ch, s], pc.at(z=pc.zh * 4 + group(s))).start()
        for d in (1, 3, 2):
            rdma(mine, mine, y_ss, y_rs.at[ch, 0], pc.at(y=lax.rem(pc.y + d, 4))).start()
    mine = feats.at[pc.row]
    far_row = (1 - pc.zh) * 4 + pc.x
    rdma(mine, mine, f_ss.at[0], f_rs.at[0], pc.at(z=lax.rem(pc.z + 4, 8))).start()

    all_self.start(jnp.dot(grad_t[...], nf_ref[...], preferred_element_type=F32))

    def apply_mask(s):
        adj_copy(s).wait()

        def tile(t, _):
            row = group(s) * 8 + t
            rows = pl.ds(pl.multiple_of(row * 128, 128), 128)
            adj[rows, :] = adj[rows, :] * wide_mask[pl.ds(row, 1), :].astype(BF16)
            return _

        lax.fori_loop(0, 8, tile, 0)

    def forward_z(ch):
        for s in range(1, 4):
            block = gath.at[ch, group(s), pc.k, pc.y]
            pc.wait_recv(block, z_rs.at[ch, s])
            for d in (1, 3, 2):
                rdma(block, block, y_ss, y_rs.at[ch, s], pc.at(y=lax.rem(pc.y + d, 4))).start()

    def multiply(ch, s):
        g = group(s)
        pc.wait_recv(gath.at[ch, g, pc.k, pl.ds(0, 3)], y_rs.at[ch, s])
        mine = gath.at[ch, g, pc.k]
        rdma(mine, mine, k_ss, k_rs.at[ch, s], pc.at(k=1 - pc.k)).start()
        pc.wait_recv(gath.at[ch, g, 1 - pc.k], k_rs.at[ch, s])
        for y in range(4):
            for k in range(2):
                lhs[:, (2 * y + k) * 128 : (2 * y + k + 1) * 128] = gath[ch, g, k, y]

        def columns(n, _):
            lanes = pl.ds(pl.multiple_of(n * 256, 256), 256)
            rows = pl.ds(pl.multiple_of(g * 1024, 1024), 1024)
            term = jnp.dot(lhs[...], adj[rows, lanes], preferred_element_type=F32)
            acc[:, lanes] = term if s == 0 else acc[:, lanes] + term
            return _

        lax.fori_loop(0, 4, columns, 0)

    def send_rows(ch):
        for r in range(8):
            part[ch, r % 4, r // 4] = acc[:, r * 128 : (r + 1) * 128].astype(BF16)
        for d in (1, 3, 2):
            x = lax.rem(pc.x + d, 4)
            rdma(part.at[ch, x], rx.at[ch, d - 1], b_ss.at[ch, 0], b_rs.at[ch, 0], pc.at(x=x)).start()

    def neigh(ch):
        all_rows = jnp.concatenate([part[ch, r % 4, r // 4] for r in range(8)], axis=1)
        all_neigh[ch].start(jnp.dot(all_rows, feats[...].reshape(8 * NODE, FEAT), preferred_element_type=F32))

    def rows_over_x(ch):
        pc.wait_recv(rx.at[ch], b_rs.at[ch, 0])

        def total(zh):
            terms = [part[ch, pc.x, zh]] + [rx[ch, d, zh] for d in range(3)]
            return sum(t.astype(F32) for t in terms)

        zout[ch] = total(1 - pc.zh).astype(BF16)
        rdma(zout.at[ch], zin.at[ch], b_ss.at[ch, 1], b_rs.at[ch, 1], pc.at(z=lax.rem(pc.z + 4, 8))).start()
        own[...] = total(pc.zh)

    def rows_over_z(ch):
        pc.wait_recv(zin.at[ch], b_rs.at[ch, 1])
        pulled = (own[...] + zin[ch].astype(F32)).astype(BF16)
        ig_t[...] += jnp.dot(wn[:, ch * CHUNK : (ch + 1) * CHUNK], pulled, preferred_element_type=F32)

    apply_mask(0)
    forward_z(0)
    all_self.plane()
    apply_mask(1)
    multiply(0, 0)
    far = feats.at[far_row]
    pc.wait_recv(far, f_rs.at[0])
    for d in (1, 3, 2):
        to = pc.at(x=lax.rem(pc.x + d, 4))
        for block in (feats.at[pc.row], far):
            rdma(block, block, f_ss.at[1], f_rs.at[1], to).start()
    forward_z(1)
    all_self.column()
    apply_mask(2)
    apply_mask(3)
    multiply(0, 1)
    all_self.spread(factor)
    multiply(0, 2)
    all_self.cross()
    for copy in w_copies:
        copy.wait()
    ig_t[...] = jnp.dot(ws[...], grad_t[...], preferred_element_type=F32)
    multiply(0, 3)
    send_rows(0)
    pc.wait_recv(feats.at[pl.ds(0, 6)], f_rs.at[1])
    neigh(0)
    all_self.finish(gs_ref, 0)
    multiply(1, 0)
    all_neigh[0].plane()
    rows_over_x(0)
    multiply(1, 1)
    all_neigh[0].column()
    rows_over_z(0)
    multiply(1, 2)
    all_neigh[0].spread(factor)
    multiply(1, 3)
    send_rows(1)
    neigh(1)
    all_neigh[0].cross()
    all_neigh[1].plane()
    rows_over_x(1)
    all_neigh[1].column()
    all_neigh[0].finish(gn_ref, 0)
    rows_over_z(1)
    ig_ref[...] = ig_t[...].T.astype(BF16)
    all_neigh[1].spread(factor)
    all_neigh[1].cross()

    for _ in range(PARTS):
        pc.wait_send(gath.at[0, 0, 0, pl.ds(0, 3)], z_ss)
    for _ in range(PARTS):
        pc.wait_send(gath.at[0, pl.ds(0, 1), 0, pl.ds(0, 3)], y_ss)
        pc.wait_send(gath.at[0, pl.ds(0, 3), 0, pl.ds(0, 3)], y_ss)
        pc.wait_send(gath.at[0, :, 0], k_ss)
    pc.wait_send(feats.at[0], f_ss.at[0])
    pc.wait_send(feats.at[pl.ds(0, 6)], f_ss.at[1])
    for ch in range(PARTS):
        pc.wait_send(rx.at[ch], b_ss.at[ch, 0])
        pc.wait_send(zin.at[ch], b_ss.at[ch, 1])
    for one in sums:
        one.drain()
    all_neigh[1].finish(gn_ref, CHUNK)


def local(node_features, out_grad, adjacency, tile_mask, degrees, w_self, w_neigh):
    node_count = NODE * lax.axis_size("row") * lax.axis_size("col")
    factor = 1.0 / math.sqrt(node_count)
    vmem = pl.BlockSpec(memory_space=pltpu.VMEM)
    hbm = pl.BlockSpec(memory_space=pl.ANY)
    dma = pltpu.SemaphoreType.DMA
    scratch = [
        pltpu.VMEM((4096, 1024), BF16),
        pltpu.VMEM((32, 1024), F32),
        pltpu.VMEM((PARTS, 4, 2, 4, CHUNK, NODE), BF16),
        pltpu.VMEM((CHUNK, 1024), BF16),
        pltpu.VMEM((CHUNK, 1024), F32),
        pltpu.VMEM((PARTS, 4, 2, CHUNK, NODE), BF16),
        pltpu.VMEM((PARTS, 3, 2, CHUNK, NODE), BF16),
        pltpu.VMEM((PARTS, CHUNK, NODE), BF16),
        pltpu.VMEM((PARTS, CHUNK, NODE), BF16),
        pltpu.VMEM((CHUNK, NODE), F32),
        pltpu.VMEM((8, NODE, FEAT), BF16),
        pltpu.VMEM((FEAT, FEAT), BF16),
        pltpu.VMEM((FEAT, FEAT), BF16),
        pltpu.VMEM((FEAT, NODE), BF16),
        pltpu.VMEM((FEAT, NODE), F32),
        dma((6,)),
        dma,
        dma((PARTS, 4)),
        dma,
        dma((PARTS, 4)),
        dma,
        dma((PARTS, 4)),
        dma((2,)),
        dma((2,)),
        dma((PARTS, 2)),
        dma((PARTS, 2)),
    ]
    for rows in [FEAT] + [CHUNK] * PARTS:
        scratch += Total.scratch(rows)
    in_grad, self_t, neigh_t = pl.pallas_call(
        lambda *refs: kernel(factor, *refs),
        out_shape=(
            jax.ShapeDtypeStruct((NODE, FEAT), BF16),
            jax.ShapeDtypeStruct((FEAT, FEAT), BF16),
            jax.ShapeDtypeStruct((FEAT, FEAT), BF16),
        ),
        in_specs=[vmem, vmem, vmem, vmem, hbm, hbm, hbm],
        out_specs=(vmem, vmem, vmem),
        scratch_shapes=scratch,
        compiler_params=pltpu.CompilerParams(
            collective_id=0, has_side_effects=True, vmem_limit_bytes=56 * 1024 * 1024
        ),
    )(node_features, out_grad, tile_mask, degrees.reshape(1, NODE), adjacency, w_self, w_neigh)
    return in_grad, self_t.T.astype(F32), neigh_t.T.astype(F32)


def solution(mesh):
    in_specs = (
        P(("row", "col"), None),
        P(("row", "col"), None),
        P("row", "col"),
        P("row", "col"),
        P(("row", "col")),
        P(),
        P(),
    )
    out_specs = (P(("row", "col"), None), P(), P())
    return jax.shard_map(local, mesh=mesh, in_specs=in_specs, out_specs=out_specs, check_vma=False)
```

```python
import math

import jax
import jax.numpy as jnp
from jax import lax
from jax.experimental import pallas as pl
from jax.experimental.pallas import tpu as pltpu
from jax.sharding import PartitionSpec as P

MESH = pl.DeviceIdType.MESH
F32, BF16 = jnp.float32, jnp.bfloat16
FEAT = 512
NODE = 128
SIZES = (256, 256)
STARTS = (0, 256)
PARTS = 2
HALF = NODE // 2
SUMS = ((512, "x", "y"), (SIZES[0], "xy", None), (SIZES[1], "xy", None))


def scoped(name):
    def wrap(fn):
        def call(*args):
            with jax.named_scope(name):
                return fn(*args)

        return call

    return wrap


def rdma(src, dst, send_sem, recv_sem, to):
    return pltpu.make_async_remote_copy(
        src_ref=src, dst_ref=dst, send_sem=send_sem, recv_sem=recv_sem, device_id=to, device_id_type=MESH
    )


class Place:
    def __init__(self):
        row, col = lax.axis_index("row"), lax.axis_index("col")
        self.row, self.col = row, col
        self.x, self.zh = lax.rem(row, 4), lax.div(row, 4)
        self.zl, self.y, self.k = lax.div(col, 8), lax.rem(lax.div(col, 2), 4), lax.rem(col, 2)
        self.z = self.zh * 4 + self.zl
        self.q = self.x * 4 + self.y

    def at(self, x=None, y=None, z=None, k=None):
        x = self.x if x is None else x
        y = self.y if y is None else y
        z = self.z if z is None else z
        k = self.k if k is None else k
        return (lax.div(z, 4) * 4 + x, lax.rem(z, 4) * 8 + y * 2 + k)

    def chip(self, d):
        q = lax.rem(self.q + d, 16)
        return lax.div(q, 4), lax.rem(q, 4)

    def along(self, axis, d):
        size = 8 if axis == "z" else 4
        c = lax.rem(getattr(self, axis) + d, size)
        return c, self.at(**{axis: c})

    def wait_recv(self, ref, sem):
        rdma(ref, ref, sem, sem, self.at()).wait_recv()

    def wait_send(self, ref, sem):
        rdma(ref, ref, sem, sem, self.at()).wait_send()


class Total:
    def __init__(self, place, rows, first, second, factor, refs):
        self.place, self.rows, self.first, self.second, self.factor = place, rows, first, second, factor
        self.part, self.kin, self.out, self.in_a, self.mid, self.in_b, self.zbuf, self.whole, self.ss, self.rs = refs
        if second is None:
            self.a, self.b = place.x, place.y
        else:
            self.a, self.b = getattr(place, first), getattr(place, second)

    @staticmethod
    def scratch(rows):
        piece = (rows // 8, 128)
        return [
            pltpu.VMEM((2, rows // 2, FEAT), BF16),
            pltpu.VMEM((rows // 2, FEAT), BF16),
            pltpu.VMEM((4, 4) + piece, BF16),
            pltpu.VMEM((16,) + piece, BF16),
            pltpu.VMEM((4,) + piece, BF16),
            pltpu.VMEM((4,) + piece, BF16),
            pltpu.VMEM((8,) + piece, BF16),
            pltpu.VMEM((2, 4, 4) + piece, BF16),
            pltpu.SemaphoreType.DMA((7,)),
            pltpu.SemaphoreType.DMA((7,)),
        ]

    def spot(self, i, j):
        tall = self.rows // 8
        return slice(i * tall, (i + 1) * tall), slice(j * 128, (j + 1) * 128)

    def copy(self, n, src, dst, to):
        rdma(src, dst, self.ss.at[n], self.rs.at[n], to).start()

    @scoped("sum_start")
    def start(self):
        other = 1 - self.place.k
        self.copy(0, self.part.at[other], self.kin, self.place.at(k=other))

    @scoped("sum_first")
    def scatter(self):
        pc = self.place
        pc.wait_recv(self.kin, self.rs.at[0])
        both = (self.part[pc.k].astype(F32) + self.kin[...].astype(F32)).astype(BF16)
        for i in range(4):
            for j in range(4):
                self.out[i, j] = both[self.spot(i, j)]
        if self.second is None:

            def send(d, _):
                x, y = pc.chip(d)
                self.copy(1, self.out.at[x, y], self.in_a.at[pc.q], pc.at(x=x, y=y))
                return _

            lax.fori_loop(1, 16, send, 0)
            self.in_a[pc.q] = self.out[self.a, self.b]
        else:
            for d in (1, 3, 2):
                c, to = pc.along(self.first, d)
                self.copy(1, self.out.at[c], self.in_a.at[pl.ds(4 * self.a, 4)], to)
            self.in_a[pl.ds(4 * self.a, 4)] = self.out[self.a]

    @scoped("sum_second")
    def scatter_second(self):
        pc = self.place
        pc.wait_recv(self.in_a.at[pl.ds(0, 12)], self.rs.at[1])
        self.mid[...] = sum(self.in_a[4 * i : 4 * i + 4].astype(F32) for i in range(4)).astype(BF16)
        for d in (1, 3, 2):
            c, to = pc.along(self.second, d)
            self.copy(2, self.mid.at[c], self.in_b.at[self.b], to)
        self.in_b[self.b] = self.mid[self.b]

    @scoped("sum_column")
    def column(self):
        pc = self.place
        if self.second is None:
            self.wait_15(pc.wait_recv, self.rs.at[1])
            total = jnp.sum(self.in_a[...].astype(F32), axis=0)
        else:
            pc.wait_recv(self.in_b.at[pl.ds(0, 3)], self.rs.at[2])
            total = jnp.sum(self.in_b[...].astype(F32), axis=0)
        self.zbuf[pc.z] = total.astype(BF16)

        def send(d, _):
            self.copy(3, self.zbuf.at[pc.z], self.zbuf.at[pc.z], pc.along("z", d)[1])
            return _

        lax.fori_loop(1, 8, send, 0)

    def wait_15(self, wait, sem):
        wait(self.in_a.at[pl.ds(0, 15)], sem)

    @scoped("sum_spread")
    def spread(self):
        pc = self.place
        pc.wait_recv(self.zbuf.at[pl.ds(0, 7)], self.rs.at[3])
        self.whole[pc.k, self.a, self.b] = (jnp.sum(self.zbuf[...].astype(F32), axis=0) * self.factor).astype(BF16)
        mine = self.whole.at[pc.k, self.a, self.b]
        if self.second is None:

            def send(d, _):
                x, y = pc.chip(d)
                self.copy(4, mine, mine, pc.at(x=x, y=y))
                return _

            lax.fori_loop(1, 16, send, 0)
        else:
            for d in (1, 3, 2):
                self.copy(4, mine, mine, pc.along(self.second, d)[1])

    @scoped("sum_spread_first")
    def spread_first(self):
        pc = self.place
        pc.wait_recv(self.in_b.at[pl.ds(0, 3)], self.rs.at[4])
        mine = self.whole.at[pc.k, self.a]
        for d in (1, 3, 2):
            self.copy(5, mine, mine, pc.along(self.first, d)[1])

    @scoped("sum_cross")
    def cross(self):
        pc = self.place
        if self.second is None:
            self.wait_15(pc.wait_recv, self.rs.at[4])
        else:
            pc.wait_recv(self.in_a.at[pl.ds(0, 12)], self.rs.at[5])
        mine = self.whole.at[pc.k]
        self.copy(6, mine, mine, pc.at(k=1 - pc.k))

    @scoped("sum_finish")
    def finish(self, out_ref, base):
        pc, half = self.place, self.rows // 2
        pc.wait_recv(self.whole.at[0], self.rs.at[6])
        for h in range(2):
            for i in range(4):
                for j in range(4):
                    rows, lanes = self.spot(i, j)
                    at = base + h * half
                    out_ref[at + rows.start : at + rows.stop, lanes] = self.whole[h, i, j]

    @scoped("sum_drain")
    def drain(self):
        pc = self.place
        pc.wait_send(self.kin, self.ss.at[0])
        pc.wait_send(self.zbuf.at[pl.ds(0, 7)], self.ss.at[3])
        pc.wait_send(self.whole.at[0], self.ss.at[6])
        if self.second is None:
            self.wait_15(pc.wait_send, self.ss.at[1])
            self.wait_15(pc.wait_send, self.ss.at[4])
        else:
            pc.wait_send(self.in_a.at[pl.ds(0, 12)], self.ss.at[1])
            pc.wait_send(self.in_b.at[pl.ds(0, 3)], self.ss.at[2])
            pc.wait_send(self.in_b.at[pl.ds(0, 3)], self.ss.at[4])
            pc.wait_send(self.in_a.at[pl.ds(0, 12)], self.ss.at[5])


def kernel(factor, *refs):
    nf_ref, og_ref, mask_ref, deg_ref, adj_ref, ws_hbm, wn_hbm = refs[:7]
    ig_ref, gs_ref, gn_ref = refs[7:10]
    (
        adj, wide_mask, feats, ws, wn, grad_t, ig_t,
        local_sem, z_ss, z_rs, y_ss, near_rs, far_rs, k_ss, k_rs, f_ss, f_rs, b_ss, b_rs,
    ) = refs[10:29]
    gath, acc, part, rx, zout, zin, own = [refs[29 + i : 43 + i : 7] for i in range(7)]
    rest = refs[43:]
    pc = Place()
    all_self, early, late = [Total(pc, *spec, factor, rest[10 * i : 10 * i + 10]) for i, spec in enumerate(SUMS)]

    barrier = pltpu.get_barrier_semaphore()

    def hello(to):
        pl.semaphore_signal(barrier, inc=1, device_id=to, device_id_type=MESH)

    def hello_z(d, _):
        hello(pc.along("z", d)[1])
        return _

    def hello_plane(d, _):
        x, y = pc.chip(d)
        hello(pc.at(x=x, y=y))
        return _

    lax.fori_loop(1, 8, hello_z, 0)
    lax.fori_loop(1, 16, hello_plane, 0)
    hello(pc.at(k=1 - pc.k))

    def group(s):
        return jnp.bitwise_xor(pc.zl, s)

    def adj_copy(s):
        rows = pl.ds(pl.multiple_of(group(s) * 1024, 1024), 1024)
        return pltpu.make_async_copy(adj_ref.at[rows], adj.at[rows], local_sem.at[s])

    w_copies = [pltpu.make_async_copy(ws_hbm, ws, local_sem.at[4]), pltpu.make_async_copy(wn_hbm, wn, local_sem.at[5])]
    for s in range(4):
        adj_copy(s).start()
    for copy in w_copies:
        copy.start()

    turned = og_ref[...].astype(F32).T
    grad_t[...] = turned.astype(BF16)
    scaled_t = (turned / deg_ref[...].astype(F32)).astype(BF16)
    for ch in range(PARTS):
        gath[ch][pc.zl, pc.k, pc.y] = scaled_t[STARTS[ch] : STARTS[ch] + SIZES[ch]]
    feats[pc.row] = nf_ref[...]
    lane_tile = lax.div(lax.broadcasted_iota(jnp.int32, (8, 1024), 1), 128)
    pick = (lane_tile == lax.broadcasted_iota(jnp.int32, (8, 1024), 0)).astype(F32).astype(BF16)
    wide_mask[...] = jnp.dot(mask_ref[...].astype(F32).T.astype(BF16), pick, preferred_element_type=F32)

    def own_sum():
        value = jnp.dot(grad_t[...], nf_ref[...], preferred_element_type=F32).astype(BF16)
        all_self.part[0] = value[: FEAT // 2]
        all_self.part[1] = value[FEAT // 2 :]

    @scoped("apply_mask")
    def apply_mask(s):
        adj_copy(s).wait()

        def tile(t, _):
            row = group(s) * 8 + t
            rows = pl.ds(pl.multiple_of(row * 128, 128), 128)
            adj[rows, :] = adj[rows, :] * wide_mask[pl.ds(row, 1), :].astype(BF16)
            return _

        lax.fori_loop(0, 8, tile, 0)

    with jax.named_scope("greeting"):
        pl.semaphore_wait(barrier, 23)


    up, up_to = pc.along("y", 1)
    down, down_to = pc.along("y", 3)
    far_y = lax.rem(pc.y + 2, 4)

    def near(ch, s):
        block = gath[ch].at[group(s), pc.k, pc.y]
        rdma(block, block, y_ss, near_rs.at[ch, s], up_to).start()
        rdma(block, block, y_ss, near_rs.at[ch, s], down_to).start()

    @scoped("stage_near")
    def stage_near(ch, s):
        if s > 0:
            pc.wait_recv(gath[ch].at[group(s), pc.k, pc.y], z_rs.at[ch, s])
            near(ch, s)

    @scoped("stage_far")
    def stage_far(ch, s):
        pc.wait_recv(gath[ch].at[group(s), pc.k, pl.ds(0, 2)], near_rs.at[ch, s])
        low = gath[ch].at[group(s), pc.k, down, pl.ds(0, SIZES[ch] // 2)]
        high = gath[ch].at[group(s), pc.k, up, pl.ds(SIZES[ch] // 2, SIZES[ch] // 2)]
        rdma(low, low, y_ss, far_rs.at[ch, s], up_to).start()
        rdma(high, high, y_ss, far_rs.at[ch, s], down_to).start()

    @scoped("stage_core")
    def stage_core(ch, s):
        pc.wait_recv(gath[ch].at[group(s), pc.k, far_y], far_rs.at[ch, s])
        mine = gath[ch].at[group(s), pc.k]
        rdma(mine, mine, k_ss, k_rs.at[ch, s], pc.at(k=1 - pc.k)).start()

    @scoped("multiply")
    def multiply(ch, s):
        g = group(s)
        pc.wait_recv(gath[ch].at[g, 1 - pc.k], k_rs.at[ch, s])
        with jax.named_scope("dot"):
            rows = pl.ds(pl.multiple_of(g * 1024, 1024), 1024)
            left = jnp.concatenate([gath[ch][g, k, y] for y in range(4) for k in range(2)], axis=1)

            def columns(n, _):
                lanes = pl.ds(pl.multiple_of(n * 256, 256), 256)
                term = jnp.dot(left, adj[rows, lanes], preferred_element_type=F32)
                acc[ch][:, lanes] = term if s == 0 else acc[ch][:, lanes] + term
                return _

            lax.fori_loop(0, 4, columns, 0)

    items = [(ch, 0) for ch in range(PARTS)] + [(ch, s) for ch in range(PARTS) for s in range(1, 4)]

    @scoped("z_sends")
    def z_sends(ch):
        mine = gath[ch].at[pc.zl, pc.k, pc.y]
        for s in range(1, 4):
            rdma(mine, mine, z_ss, z_rs.at[ch, s], pc.at(z=pc.zh * 4 + group(s))).start()

    far_row = (1 - pc.zh) * 4 + pc.x
    right, right_to = pc.along("x", 1)
    left_x, left_to = pc.along("x", 3)

    @scoped("feats")
    def feats_near(n, row):
        block = feats.at[row]
        rdma(block, block, f_ss, f_rs.at[n], right_to).start()
        rdma(block, block, f_ss, f_rs.at[n], left_to).start()

    @scoped("feats")
    def feats_far(n, zh):
        pc.wait_recv(feats.at[pl.ds(0, 2)], f_rs.at[n])
        low = feats.at[zh * 4 + left_x, pl.ds(0, HALF)]
        high = feats.at[zh * 4 + right, pl.ds(HALF, HALF)]
        rdma(low, low, f_ss, f_rs.at[n + 1], right_to).start()
        rdma(high, high, f_ss, f_rs.at[n + 1], left_to).start()

    @scoped("send_rows")
    def send_rows(ch):
        for r in range(8):
            part[ch][r % 4, r // 4] = acc[ch][:, r * 128 : (r + 1) * 128].astype(BF16)

    @scoped("rows_x_start")
    def rows_x_start(ch):
        for d in (1, 3, 2):
            x, to = pc.along("x", d)
            rdma(part[ch].at[x], rx[ch].at[d - 1], b_ss.at[ch, 0], b_rs.at[ch, 0], to).start()

    @scoped("neigh")
    def neigh(ch):
        left = jnp.concatenate([part[ch][r % 4, r // 4] for r in range(8)], axis=1)
        value = jnp.dot(left, feats[...].reshape(8 * NODE, FEAT), preferred_element_type=F32)
        total = (early, late)[ch]
        total.part[0] = value[: SIZES[ch] // 2].astype(BF16)
        total.part[1] = value[SIZES[ch] // 2 :].astype(BF16)
        total.start()

    @scoped("rows_over_x")
    def rows_over_x(ch):
        pc.wait_recv(rx[ch], b_rs.at[ch, 0])

        def total(zh):
            terms = [part[ch][pc.x, zh]] + [rx[ch][d, zh] for d in range(3)]
            return sum(t.astype(F32) for t in terms)

        zout[ch][...] = total(1 - pc.zh).astype(BF16)
        rdma(zout[ch], zin[ch], b_ss.at[ch, 1], b_rs.at[ch, 1], pc.along("z", 4)[1]).start()
        own[ch][...] = total(pc.zh)

    @scoped("rows_over_z")
    def rows_over_z(ch):
        pc.wait_recv(zin[ch], b_rs.at[ch, 1])
        pulled = (own[ch][...] + zin[ch][...].astype(F32)).astype(BF16)
        ig_t[...] += jnp.dot(wn[:, STARTS[ch] : STARTS[ch] + SIZES[ch]], pulled, preferred_element_type=F32)

    @scoped("own_term")
    def own_term():
        for copy in w_copies:
            copy.wait()
        ig_t[...] = jnp.dot(ws[...], grad_t[...], preferred_element_type=F32)

    def to_far_z():
        mine = feats.at[pc.row]
        rdma(mine, mine, f_ss, f_rs.at[0], pc.along("z", 4)[1]).start()

    def from_far_z():
        pc.wait_recv(feats.at[far_row], f_rs.at[0])
        feats_near(3, far_row)

    def feats_wait():
        pc.wait_recv(feats.at[0], f_rs.at[2])
        pc.wait_recv(feats.at[0], f_rs.at[4])

    def close(ch):
        send_rows(ch)
        neigh(ch)

    def far(i):
        stage_far(*items[i])

    def forward(i):
        stage_near(*items[i])

    def core(i):
        stage_core(*items[i])

    def dot(i):
        multiply(*items[i])

    near(0, 0)
    z_sends(0)
    near(1, 0)
    feats_near(1, pc.row)
    own_sum()
    all_self.start()
    apply_mask(0)
    far(0)
    far(1)
    forward(2)
    core(0)
    forward(3)
    core(1)
    forward(4)
    to_far_z()
    z_sends(1)
    dot(0)
    far(2)
    all_self.scatter()
    dot(1)
    far(3)
    apply_mask(1)
    feats_far(1, pc.zh)
    core(2)
    far(4)
    apply_mask(2)
    apply_mask(3)
    dot(2)
    core(3)
    forward(5)
    all_self.scatter_second()
    core(4)
    dot(3)
    from_far_z()
    forward(6)
    far(5)
    own_term()
    dot(4)
    forward(7)
    send_rows(0)
    rows_x_start(0)
    core(5)
    all_self.column()
    far(6)
    feats_far(3, 1 - pc.zh)
    dot(5)
    far(7)
    core(6)
    feats_wait()
    neigh(0)
    core(7)
    dot(6)
    early.scatter()
    all_self.spread()
    rows_over_x(0)
    dot(7)
    send_rows(1)
    neigh(1)
    all_self.spread_first()
    late.scatter()
    rows_x_start(1)
    early.column()
    rows_over_z(0)
    all_self.cross()
    late.column()
    early.spread()
    all_self.finish(gs_ref, 0)
    late.spread()
    rows_over_x(1)
    early.cross()
    late.cross()
    early.finish(gn_ref, 0)
    rows_over_z(1)
    ig_ref[...] = ig_t[...].T.astype(BF16)
    late.finish(gn_ref, STARTS[1])

    with jax.named_scope("drain"):
        for blocks in gath:
            pc.wait_send(blocks.at[pl.ds(0, 3), 0, 0], z_ss)
            pc.wait_send(blocks.at[pl.ds(0, 3), 0], y_ss)
            pc.wait_send(blocks.at[:, 0], k_ss)
        pc.wait_send(feats.at[pl.ds(0, 7)], f_ss)
        for ch in range(PARTS):
            pc.wait_send(rx[ch], b_ss.at[ch, 0])
            pc.wait_send(zin[ch], b_ss.at[ch, 1])
        for total in (all_self, early, late):
            total.drain()


def finish_kernel(ig_ref, gs_ref, gn_ref, ig_out, gs_out, gn_out):
    ig_out[...] = ig_ref[...]
    gs_out[...] = gs_ref[...].astype(F32).T
    gn_out[...] = gn_ref[...].astype(F32).T


def local(node_features, out_grad, adjacency, tile_mask, degrees, w_self, w_neigh):
    node_count = NODE * lax.axis_size("row") * lax.axis_size("col")
    factor = 1.0 / math.sqrt(node_count)
    vmem = pl.BlockSpec(memory_space=pltpu.VMEM)
    hbm = pl.BlockSpec(memory_space=pl.ANY)
    dma = pltpu.SemaphoreType.DMA
    scratch = [
        pltpu.VMEM((4096, 1024), BF16),
        pltpu.VMEM((32, 1024), F32),
        pltpu.VMEM((8, NODE, FEAT), BF16),
        pltpu.VMEM((FEAT, FEAT), BF16),
        pltpu.VMEM((FEAT, FEAT), BF16),
        pltpu.VMEM((FEAT, NODE), BF16),
        pltpu.VMEM((FEAT, NODE), F32),
        dma((6,)),
        dma,
        dma((PARTS, 4)),
        dma,
        dma((PARTS, 4)),
        dma((PARTS, 4)),
        dma,
        dma((PARTS, 4)),
        dma,
        dma((5,)),
        dma((PARTS, 2)),
        dma((PARTS, 2)),
    ]
    for size in SIZES:
        scratch += [
            pltpu.VMEM((4, 2, 4, size, NODE), BF16),
            pltpu.VMEM((size, 1024), F32),
            pltpu.VMEM((4, 2, size, NODE), BF16),
            pltpu.VMEM((3, 2, size, NODE), BF16),
            pltpu.VMEM((size, NODE), BF16),
            pltpu.VMEM((size, NODE), BF16),
            pltpu.VMEM((size, NODE), F32),
        ]
    for rows, _, _ in SUMS:
        scratch += Total.scratch(rows)
    shapes = [pltpu.VMEM((n, FEAT), BF16) for n in (NODE, FEAT, FEAT)]
    results = pl.pallas_call(
        lambda *refs: kernel(factor, *refs),
        out_shape=shapes,
        in_specs=[vmem, vmem, vmem, vmem, hbm, hbm, hbm],
        out_specs=(vmem, vmem, vmem),
        scratch_shapes=scratch,
        compiler_params=pltpu.CompilerParams(
            collective_id=0, has_side_effects=True, vmem_limit_bytes=56 * 1024 * 1024
        ),
    )(node_features, out_grad, tile_mask.T, degrees.reshape(1, NODE), adjacency, w_self, w_neigh)
    return pl.pallas_call(
        finish_kernel,
        out_shape=[jax.ShapeDtypeStruct((n, FEAT), t) for n, t in ((NODE, BF16), (FEAT, F32), (FEAT, F32))],
        in_specs=[vmem] * 3,
        out_specs=[vmem] * 3,
        compiler_params=pltpu.CompilerParams(vmem_limit_bytes=16 * 1024 * 1024),
    )(*results)


def solution(mesh):
    in_specs = (
        P(("row", "col"), None),
        P(("row", "col"), None),
        P("row", "col"),
        P("row", "col"),
        P(("row", "col")),
        P(),
        P(),
    )
    out_specs = (P(("row", "col"), None), P(), P())
    return jax.shard_map(local, mesh=mesh, in_specs=in_specs, out_specs=out_specs, check_vma=False)
```

```python
import math

import jax
import jax.numpy as jnp
from jax import lax
from jax.experimental import pallas as pl
from jax.experimental.pallas import tpu as pltpu
from jax.sharding import PartitionSpec as P

MESH = pl.DeviceIdType.MESH
F32, BF16 = jnp.float32, jnp.bfloat16
FEAT = 512
NODE = 128
SIZES = (256, 256)
STARTS = (0, 256)
PARTS = 2
HALF = NODE // 2
SUMS = ((512, "x", "y", True), (SIZES[0], "xy", None, False), (SIZES[1], "xy", None, False))


def scoped(name):
    def wrap(fn):
        def call(*args):
            with jax.named_scope(name):
                return fn(*args)

        return call

    return wrap


def rdma(src, dst, send_sem, recv_sem, to):
    return pltpu.make_async_remote_copy(
        src_ref=src, dst_ref=dst, send_sem=send_sem, recv_sem=recv_sem, device_id=to, device_id_type=MESH
    )


class Place:
    def __init__(self):
        row, col = lax.axis_index("row"), lax.axis_index("col")
        self.row, self.col = row, col
        self.x, self.zh = lax.rem(row, 4), lax.div(row, 4)
        self.zl, self.y, self.k = lax.div(col, 8), lax.rem(lax.div(col, 2), 4), lax.rem(col, 2)
        self.z = self.zh * 4 + self.zl
        self.q = self.x * 4 + self.y

    def at(self, x=None, y=None, z=None, k=None):
        x = self.x if x is None else x
        y = self.y if y is None else y
        z = self.z if z is None else z
        k = self.k if k is None else k
        return (lax.div(z, 4) * 4 + x, lax.rem(z, 4) * 8 + y * 2 + k)

    def chip(self, d):
        q = lax.rem(self.q + d, 16)
        return lax.div(q, 4), lax.rem(q, 4)

    def along(self, axis, d):
        size = 8 if axis == "z" else 4
        c = lax.rem(getattr(self, axis) + d, size)
        return c, self.at(**{axis: c})

    def wait_recv(self, ref, sem):
        rdma(ref, ref, sem, sem, self.at()).wait_recv()

    def wait_send(self, ref, sem):
        rdma(ref, ref, sem, sem, self.at()).wait_send()


class Total:
    def __init__(self, place, rows, first, second, turn, factor, refs):
        self.place, self.rows, self.first, self.second, self.turn, self.factor = place, rows, first, second, turn, factor
        self.part, self.kin, self.out, self.in_a, self.mid, self.in_b, self.zbuf, self.whole, self.ss, self.rs = refs
        if second is None:
            self.a, self.b = place.x, place.y
        else:
            self.a, self.b = getattr(place, first), getattr(place, second)

    @staticmethod
    def scratch(rows):
        piece = (rows // 8, 128)
        return [
            pltpu.VMEM((2, rows // 2, FEAT), BF16),
            pltpu.VMEM((rows // 2, FEAT), BF16),
            pltpu.VMEM((4, 4) + piece, BF16),
            pltpu.VMEM((16,) + piece, BF16),
            pltpu.VMEM((4,) + piece, BF16),
            pltpu.VMEM((4,) + piece, BF16),
            pltpu.VMEM((8,) + piece, BF16),
            pltpu.VMEM((2, 4, 4) + piece, BF16),
            pltpu.SemaphoreType.DMA((7,)),
            pltpu.SemaphoreType.DMA((7,)),
        ]

    def spot(self, i, j):
        tall = self.rows // 8
        return slice(i * tall, (i + 1) * tall), slice(j * 128, (j + 1) * 128)

    def copy(self, n, src, dst, to):
        rdma(src, dst, self.ss.at[n], self.rs.at[n], to).start()

    @scoped("sum_start")
    def start(self):
        other = 1 - self.place.k
        self.copy(0, self.part.at[other], self.kin, self.place.at(k=other))

    @scoped("sum_first")
    def scatter(self):
        pc = self.place
        pc.wait_recv(self.kin, self.rs.at[0])
        both = (self.part[pc.k].astype(F32) + self.kin[...].astype(F32)).astype(BF16)
        for i in range(4):
            for j in range(4):
                self.out[i, j] = both[self.spot(i, j)]
        if self.second is None:

            def send(d, _):
                x, y = pc.chip(d)
                self.copy(1, self.out.at[x, y], self.in_a.at[pc.q], pc.at(x=x, y=y))
                return _

            lax.fori_loop(1, 16, send, 0)
            self.in_a[pc.q] = self.out[self.a, self.b]
        else:
            for d in (1, 3, 2):
                c, to = pc.along(self.first, d)
                self.copy(1, self.out.at[c], self.in_a.at[pl.ds(4 * self.a, 4)], to)
            self.in_a[pl.ds(4 * self.a, 4)] = self.out[self.a]

    @scoped("sum_second")
    def scatter_second(self):
        pc = self.place
        pc.wait_recv(self.in_a.at[pl.ds(0, 12)], self.rs.at[1])
        self.mid[...] = sum(self.in_a[4 * i : 4 * i + 4].astype(F32) for i in range(4)).astype(BF16)
        for d in (1, 3, 2):
            c, to = pc.along(self.second, d)
            self.copy(2, self.mid.at[c], self.in_b.at[self.b], to)
        self.in_b[self.b] = self.mid[self.b]

    @scoped("sum_column")
    def column(self):
        pc = self.place
        if self.second is None:
            self.wait_15(pc.wait_recv, self.rs.at[1])
            total = jnp.sum(self.in_a[...].astype(F32), axis=0)
        else:
            pc.wait_recv(self.in_b.at[pl.ds(0, 3)], self.rs.at[2])
            total = jnp.sum(self.in_b[...].astype(F32), axis=0)
        self.zbuf[pc.z] = total.astype(BF16)

        def send(d, _):
            self.copy(3, self.zbuf.at[pc.z], self.zbuf.at[pc.z], pc.along("z", d)[1])
            return _

        lax.fori_loop(1, 8, send, 0)

    def wait_15(self, wait, sem):
        wait(self.in_a.at[pl.ds(0, 15)], sem)

    @scoped("sum_spread")
    def spread(self):
        pc = self.place
        pc.wait_recv(self.zbuf.at[pl.ds(0, 7)], self.rs.at[3])
        self.whole[pc.k, self.a, self.b] = (jnp.sum(self.zbuf[...].astype(F32), axis=0) * self.factor).astype(BF16)
        mine = self.whole.at[pc.k, self.a, self.b]
        if self.second is None:

            def send(d, _):
                x, y = pc.chip(d)
                self.copy(4, mine, mine, pc.at(x=x, y=y))
                return _

            lax.fori_loop(1, 16, send, 0)
        else:
            for d in (1, 3, 2):
                self.copy(4, mine, mine, pc.along(self.first if self.turn else self.second, d)[1])

    @scoped("sum_spread_first")
    def spread_first(self):
        pc = self.place
        pc.wait_recv(self.in_b.at[pl.ds(0, 3)], self.rs.at[4])
        mine = self.whole.at[pc.k, :, self.b] if self.turn else self.whole.at[pc.k, self.a]
        for d in (1, 3, 2):
            self.copy(5, mine, mine, pc.along(self.second if self.turn else self.first, d)[1])

    @scoped("sum_cross")
    def cross(self):
        pc = self.place
        if self.second is None:
            self.wait_15(pc.wait_recv, self.rs.at[4])
        else:
            pc.wait_recv(self.in_a.at[pl.ds(0, 12)], self.rs.at[5])
        mine = self.whole.at[pc.k]
        self.copy(6, mine, mine, pc.at(k=1 - pc.k))

    @scoped("sum_finish")
    def finish(self, out_ref, base):
        pc, half = self.place, self.rows // 2
        pc.wait_recv(self.whole.at[0], self.rs.at[6])
        for h in range(2):
            for i in range(4):
                for j in range(4):
                    rows, lanes = self.spot(i, j)
                    at = base + h * half
                    out_ref[at + rows.start : at + rows.stop, lanes] = self.whole[h, i, j]

    @scoped("sum_drain")
    def drain(self):
        pc = self.place
        pc.wait_send(self.kin, self.ss.at[0])
        pc.wait_send(self.zbuf.at[pl.ds(0, 7)], self.ss.at[3])
        pc.wait_send(self.whole.at[0], self.ss.at[6])
        if self.second is None:
            self.wait_15(pc.wait_send, self.ss.at[1])
            self.wait_15(pc.wait_send, self.ss.at[4])
        else:
            pc.wait_send(self.in_a.at[pl.ds(0, 12)], self.ss.at[1])
            pc.wait_send(self.in_b.at[pl.ds(0, 3)], self.ss.at[2])
            pc.wait_send(self.in_b.at[pl.ds(0, 3)], self.ss.at[4])
            pc.wait_send(self.in_a.at[pl.ds(0, 12)], self.ss.at[5])


def kernel(factor, *refs):
    nf_hbm, og_hbm, mask_hbm, deg_hbm, adj_ref, ws_hbm, wn_hbm = refs[:7]
    ig_ref, gs_ref, gn_ref = refs[7:10]
    (
        adj, wide_mask, feats, ws, wn, grad_t, ig_t, og_ref, mask_ref, deg_ref,
        local_sem, z_ss, z_rs, y_ss, near_rs, far_rs, k_ss, k_rs, f_ss, f_rs, b_ss, b_rs,
    ) = refs[10:32]
    gath, acc, part, rx, zout, zin, own = [refs[32 + i : 46 + i : 7] for i in range(7)]
    rest = refs[46:]
    pc = Place()
    all_self, early, late = [Total(pc, *spec, factor, rest[10 * i : 10 * i + 10]) for i, spec in enumerate(SUMS)]

    barrier = pltpu.get_barrier_semaphore()

    def hello(to):
        pl.semaphore_signal(barrier, inc=1, device_id=to, device_id_type=MESH)

    def hello_z(d, _):
        hello(pc.along("z", d)[1])
        return _

    def hello_plane(d, _):
        x, y = pc.chip(d)
        hello(pc.at(x=x, y=y))
        return _

    lax.fori_loop(1, 8, hello_z, 0)
    lax.fori_loop(1, 16, hello_plane, 0)
    hello(pc.at(k=1 - pc.k))

    def group(s):
        return jnp.bitwise_xor(pc.zl, s)

    def adj_copy(s):
        rows = pl.ds(pl.multiple_of(group(s) * 1024, 1024), 1024)
        return pltpu.make_async_copy(adj_ref.at[rows], adj.at[rows], local_sem.at[s])

    w_copies = [pltpu.make_async_copy(ws_hbm, ws, local_sem.at[4]), pltpu.make_async_copy(wn_hbm, wn, local_sem.at[5])]
    small = [(og_hbm, og_ref), (deg_hbm, deg_ref), (nf_hbm, feats.at[pc.row]), (mask_hbm, mask_ref)]
    in_copies = [pltpu.make_async_copy(src, dst, local_sem.at[6 + i]) for i, (src, dst) in enumerate(small)]
    for copy in in_copies:
        copy.start()
    for s in range(4):
        adj_copy(s).start()
    for copy in w_copies:
        copy.start()
    in_copies[0].wait()
    in_copies[1].wait()

    turned = og_ref[...].astype(F32).T
    grad_t[...] = turned.astype(BF16)
    scaled_t = (turned / deg_ref[...].astype(F32)).astype(BF16)
    for ch in range(PARTS):
        gath[ch][pc.zl, pc.k, pc.y] = scaled_t[STARTS[ch] : STARTS[ch] + SIZES[ch]]

    def spread_mask():
        in_copies[3].wait()
        lane_tile = lax.div(lax.broadcasted_iota(jnp.int32, (8, 1024), 1), 128)
        pick = (lane_tile == lax.broadcasted_iota(jnp.int32, (8, 1024), 0)).astype(F32).astype(BF16)
        wide_mask[...] = jnp.dot(mask_ref[...].astype(F32).T.astype(BF16), pick, preferred_element_type=F32)

    def own_sum():
        value = jnp.dot(grad_t[...], feats[pc.row], preferred_element_type=F32).astype(BF16)
        all_self.part[0] = value[: FEAT // 2]
        all_self.part[1] = value[FEAT // 2 :]

    @scoped("apply_mask")
    def apply_mask(s):
        adj_copy(s).wait()

        def tile(t, _):
            row = group(s) * 8 + t
            rows = pl.ds(pl.multiple_of(row * 128, 128), 128)
            adj[rows, :] = adj[rows, :] * wide_mask[pl.ds(row, 1), :].astype(BF16)
            return _

        lax.fori_loop(0, 8, tile, 0)

    with jax.named_scope("greeting"):
        pl.semaphore_wait(barrier, 23)


    up, up_to = pc.along("y", 1)
    down, down_to = pc.along("y", 3)
    far_y = lax.rem(pc.y + 2, 4)

    def near(ch, s):
        block = gath[ch].at[group(s), pc.k, pc.y]
        for d in (1, 3, 2):
            rdma(block, block, y_ss, near_rs.at[ch, s], pc.along("y", d)[1]).start()

    @scoped("stage_near")
    def stage_near(ch, s):
        if s > 0:
            pc.wait_recv(gath[ch].at[group(s), pc.k, pc.y], z_rs.at[ch, s])
            near(ch, s)

    def stage_far(ch, s):
        pass

    @scoped("stage_core")
    def stage_core(ch, s):
        pc.wait_recv(gath[ch].at[group(s), pc.k, pl.ds(0, 3)], near_rs.at[ch, s])
        mine = gath[ch].at[group(s), pc.k]
        rdma(mine, mine, k_ss, k_rs.at[ch, s], pc.at(k=1 - pc.k)).start()

    @scoped("multiply")
    def multiply(ch, s):
        g = group(s)
        pc.wait_recv(gath[ch].at[g, 1 - pc.k], k_rs.at[ch, s])
        with jax.named_scope("dot"):
            rows = pl.ds(pl.multiple_of(g * 1024, 1024), 1024)
            left = jnp.concatenate([gath[ch][g, k, y] for y in range(4) for k in range(2)], axis=1)

            def columns(n, _):
                lanes = pl.ds(pl.multiple_of(n * 256, 256), 256)
                term = jnp.dot(left, adj[rows, lanes], preferred_element_type=F32)
                acc[ch][:, lanes] = term if s == 0 else acc[ch][:, lanes] + term
                return _

            lax.fori_loop(0, 4, columns, 0)

    items = [(ch, 0) for ch in range(PARTS)] + [(ch, s) for ch in range(PARTS) for s in range(1, 4)]

    @scoped("z_sends")
    def z_sends(ch):
        mine = gath[ch].at[pc.zl, pc.k, pc.y]
        for s in range(1, 4):
            rdma(mine, mine, z_ss, z_rs.at[ch, s], pc.at(z=pc.zh * 4 + group(s))).start()

    far_row = (1 - pc.zh) * 4 + pc.x
    right, right_to = pc.along("x", 1)
    left_x, left_to = pc.along("x", 3)

    @scoped("feats")
    def feats_near(n, row):
        block = feats.at[row]
        rdma(block, block, f_ss, f_rs.at[n], right_to).start()
        rdma(block, block, f_ss, f_rs.at[n], left_to).start()

    @scoped("feats")
    def feats_far(n, zh):
        pc.wait_recv(feats.at[pl.ds(0, 2)], f_rs.at[n])
        low = feats.at[zh * 4 + left_x, pl.ds(0, HALF)]
        high = feats.at[zh * 4 + right, pl.ds(HALF, HALF)]
        rdma(low, low, f_ss, f_rs.at[n + 1], right_to).start()
        rdma(high, high, f_ss, f_rs.at[n + 1], left_to).start()

    @scoped("send_rows")
    def send_rows(ch):
        for r in range(8):
            part[ch][r % 4, r // 4] = acc[ch][:, r * 128 : (r + 1) * 128].astype(BF16)

    @scoped("rows_x_start")
    def rows_x_start(ch):
        for d in (1, 3, 2):
            x, to = pc.along("x", d)
            rdma(part[ch].at[x], rx[ch].at[d - 1], b_ss.at[ch, 0], b_rs.at[ch, 0], to).start()

    @scoped("neigh")
    def neigh(ch):
        left = jnp.concatenate([part[ch][r % 4, r // 4] for r in range(8)], axis=1)
        value = jnp.dot(left, feats[...].reshape(8 * NODE, FEAT), preferred_element_type=F32)
        total = (early, late)[ch]
        total.part[0] = value[: SIZES[ch] // 2].astype(BF16)
        total.part[1] = value[SIZES[ch] // 2 :].astype(BF16)
        total.start()

    @scoped("rows_over_x")
    def rows_over_x(ch):
        pc.wait_recv(rx[ch], b_rs.at[ch, 0])

        def total(zh):
            terms = [part[ch][pc.x, zh]] + [rx[ch][d, zh] for d in range(3)]
            return sum(t.astype(F32) for t in terms)

        zout[ch][...] = total(1 - pc.zh).astype(BF16)
        rdma(zout[ch], zin[ch], b_ss.at[ch, 1], b_rs.at[ch, 1], pc.along("z", 4)[1]).start()
        own[ch][...] = total(pc.zh)

    @scoped("rows_over_z")
    def rows_over_z(ch):
        pc.wait_recv(zin[ch], b_rs.at[ch, 1])
        pulled = (own[ch][...] + zin[ch][...].astype(F32)).astype(BF16)
        ig_t[...] += jnp.dot(wn[:, STARTS[ch] : STARTS[ch] + SIZES[ch]], pulled, preferred_element_type=F32)

    @scoped("own_term")
    def own_term():
        for copy in w_copies:
            copy.wait()
        ig_t[...] = jnp.dot(ws[...], grad_t[...], preferred_element_type=F32)

    def to_far_z():
        mine = feats.at[pc.row]
        rdma(mine, mine, f_ss, f_rs.at[0], pc.along("z", 4)[1]).start()

    def from_far_z():
        pc.wait_recv(feats.at[far_row], f_rs.at[0])
        feats_near(3, far_row)

    def feats_wait():
        pc.wait_recv(feats.at[0], f_rs.at[2])
        pc.wait_recv(feats.at[0], f_rs.at[4])

    def close(ch):
        send_rows(ch)
        neigh(ch)

    def far(i):
        stage_far(*items[i])

    def forward(i):
        stage_near(*items[i])

    def core(i):
        stage_core(*items[i])

    def dot(i):
        multiply(*items[i])

    near(0, 0)
    z_sends(0)
    in_copies[2].wait()
    own_sum()
    all_self.start()
    spread_mask()
    apply_mask(0)
    near(1, 0)
    feats_near(1, pc.row)
    apply_mask(1)
    apply_mask(2)
    forward(2)
    core(0)
    forward(3)
    core(1)
    forward(4)
    to_far_z()
    z_sends(1)
    dot(0)
    all_self.scatter()
    core(2)
    dot(1)
    feats_far(1, pc.zh)
    core(3)
    apply_mask(3)
    dot(2)
    core(4)
    from_far_z()
    forward(5)
    all_self.scatter_second()
    dot(3)
    forward(6)
    own_term()
    dot(4)
    forward(7)
    send_rows(0)
    feats_far(3, 1 - pc.zh)
    rows_x_start(0)
    core(5)
    all_self.column()
    core(6)
    dot(5)
    feats_wait()
    neigh(0)
    core(7)
    dot(6)
    early.scatter()
    all_self.spread()
    dot(7)
    send_rows(1)
    neigh(1)
    rows_over_x(0)
    late.scatter()
    early.column()
    rows_x_start(1)
    all_self.spread_first()
    rows_over_z(0)
    late.column()
    early.spread()
    all_self.cross()
    rows_over_x(1)
    late.spread()
    early.cross()
    all_self.finish(gs_ref, 0)
    late.cross()
    early.finish(gn_ref, 0)
    rows_over_z(1)
    ig_ref[...] = ig_t[...].T.astype(BF16)
    late.finish(gn_ref, STARTS[1])

    with jax.named_scope("drain"):
        for blocks in gath:
            pc.wait_send(blocks.at[pl.ds(0, 3), 0, 0], z_ss)
            pc.wait_send(blocks.at[pl.ds(0, 3), 0], y_ss)
            pc.wait_send(blocks.at[:, 0], k_ss)
        pc.wait_send(feats.at[pl.ds(0, 7)], f_ss)
        for ch in range(PARTS):
            pc.wait_send(rx[ch], b_ss.at[ch, 0])
            pc.wait_send(zin[ch], b_ss.at[ch, 1])
        for total in (all_self, early, late):
            total.drain()


def finish_kernel(ig_ref, gs_ref, gn_ref, ig_out, gs_out, gn_out):
    ig_out[...] = ig_ref[...]
    gs_out[...] = gs_ref[...].astype(F32).T
    gn_out[...] = gn_ref[...].astype(F32).T


def local(node_features, out_grad, adjacency, tile_mask, degrees, w_self, w_neigh):
    node_count = NODE * lax.axis_size("row") * lax.axis_size("col")
    factor = 1.0 / math.sqrt(node_count)
    vmem = pl.BlockSpec(memory_space=pltpu.VMEM)
    hbm = pl.BlockSpec(memory_space=pl.ANY)
    dma = pltpu.SemaphoreType.DMA
    scratch = [
        pltpu.VMEM((4096, 1024), BF16),
        pltpu.VMEM((32, 1024), F32),
        pltpu.VMEM((8, NODE, FEAT), BF16),
        pltpu.VMEM((FEAT, FEAT), BF16),
        pltpu.VMEM((FEAT, FEAT), BF16),
        pltpu.VMEM((FEAT, NODE), BF16),
        pltpu.VMEM((FEAT, NODE), F32),
        pltpu.VMEM((NODE, FEAT), BF16),
        pltpu.VMEM((8, 32), jnp.int32),
        pltpu.VMEM((1, NODE), jnp.int32),
        dma((10,)),
        dma,
        dma((PARTS, 4)),
        dma,
        dma((PARTS, 4)),
        dma((PARTS, 4)),
        dma,
        dma((PARTS, 4)),
        dma,
        dma((5,)),
        dma((PARTS, 2)),
        dma((PARTS, 2)),
    ]
    for size in SIZES:
        scratch += [
            pltpu.VMEM((4, 2, 4, size, NODE), BF16),
            pltpu.VMEM((size, 1024), F32),
            pltpu.VMEM((4, 2, size, NODE), BF16),
            pltpu.VMEM((3, 2, size, NODE), BF16),
            pltpu.VMEM((size, NODE), BF16),
            pltpu.VMEM((size, NODE), BF16),
            pltpu.VMEM((size, NODE), F32),
        ]
    for rows, _, _, _ in SUMS:
        scratch += Total.scratch(rows)
    shapes = [pltpu.VMEM((n, FEAT), BF16) for n in (NODE, FEAT, FEAT)]
    results = pl.pallas_call(
        lambda *refs: kernel(factor, *refs),
        out_shape=shapes,
        in_specs=[hbm] * 7,
        out_specs=(vmem, vmem, vmem),
        scratch_shapes=scratch,
        compiler_params=pltpu.CompilerParams(
            collective_id=0, has_side_effects=True, vmem_limit_bytes=56 * 1024 * 1024
        ),
    )(node_features, out_grad, tile_mask.T, degrees.reshape(1, NODE), adjacency, w_self, w_neigh)
    return pl.pallas_call(
        finish_kernel,
        out_shape=[jax.ShapeDtypeStruct((n, FEAT), t) for n, t in ((NODE, BF16), (FEAT, F32), (FEAT, F32))],
        in_specs=[vmem] * 3,
        out_specs=[vmem] * 3,
        compiler_params=pltpu.CompilerParams(vmem_limit_bytes=16 * 1024 * 1024),
    )(*results)


def solution(mesh):
    in_specs = (
        P(("row", "col"), None),
        P(("row", "col"), None),
        P("row", "col"),
        P("row", "col"),
        P(("row", "col")),
        P(),
        P(),
    )
    out_specs = (P(("row", "col"), None), P(), P())
    return jax.shard_map(local, mesh=mesh, in_specs=in_specs, out_specs=out_specs, check_vma=False)
```

```python
import math

import jax
import jax.numpy as jnp
from jax import lax
from jax.experimental import pallas as pl
from jax.experimental.pallas import tpu as pltpu
from jax.sharding import PartitionSpec as P

MESH = pl.DeviceIdType.MESH
F32, BF16 = jnp.float32, jnp.bfloat16
FEAT = 512
NODE = 128
SIZES = (256, 128, 128)
STARTS = (0, 256, 384)
PARTS = 3
HALF = NODE // 2
SUMS = ((512, "x", "y", True), (384, "xy", None, False), (128, "xy", None, False))


def scoped(name):
    def wrap(fn):
        def call(*args):
            with jax.named_scope(name):
                return fn(*args)

        return call

    return wrap


def rdma(src, dst, send_sem, recv_sem, to):
    return pltpu.make_async_remote_copy(
        src_ref=src, dst_ref=dst, send_sem=send_sem, recv_sem=recv_sem, device_id=to, device_id_type=MESH
    )


class Place:
    def __init__(self):
        row, col = lax.axis_index("row"), lax.axis_index("col")
        self.row, self.col = row, col
        self.x, self.zh = lax.rem(row, 4), lax.div(row, 4)
        self.zl, self.y, self.k = lax.div(col, 8), lax.rem(lax.div(col, 2), 4), lax.rem(col, 2)
        self.z = self.zh * 4 + self.zl
        self.q = self.x * 4 + self.y

    def at(self, x=None, y=None, z=None, k=None):
        x = self.x if x is None else x
        y = self.y if y is None else y
        z = self.z if z is None else z
        k = self.k if k is None else k
        return (lax.div(z, 4) * 4 + x, lax.rem(z, 4) * 8 + y * 2 + k)

    def chip(self, d):
        q = lax.rem(self.q + d, 16)
        return lax.div(q, 4), lax.rem(q, 4)

    def along(self, axis, d):
        size = 8 if axis == "z" else 4
        c = lax.rem(getattr(self, axis) + d, size)
        return c, self.at(**{axis: c})

    def wait_recv(self, ref, sem):
        rdma(ref, ref, sem, sem, self.at()).wait_recv()

    def wait_send(self, ref, sem):
        rdma(ref, ref, sem, sem, self.at()).wait_send()


class Total:
    def __init__(self, place, rows, first, second, turn, factor, refs):
        self.place, self.rows, self.first, self.second, self.turn, self.factor = place, rows, first, second, turn, factor
        self.part, self.kin, self.out, self.in_a, self.mid, self.in_b, self.zbuf, self.whole, self.ss, self.rs = refs
        if second is None:
            self.a, self.b = place.x, place.y
        else:
            self.a, self.b = getattr(place, first), getattr(place, second)

    @staticmethod
    def scratch(rows):
        piece = (rows // 8, 128)
        return [
            pltpu.VMEM((rows, FEAT), BF16),
            pltpu.VMEM((rows // 2, FEAT), BF16),
            pltpu.VMEM((4, 4) + piece, BF16),
            pltpu.VMEM((16,) + piece, BF16),
            pltpu.VMEM((4,) + piece, BF16),
            pltpu.VMEM((4,) + piece, BF16),
            pltpu.VMEM((8,) + piece, BF16),
            pltpu.VMEM((2, 4, 4) + piece, BF16),
            pltpu.SemaphoreType.DMA((7,)),
            pltpu.SemaphoreType.DMA((7,)),
        ]

    def spot(self, i, j):
        tall = self.rows // 8
        return slice(i * tall, (i + 1) * tall), slice(j * 128, (j + 1) * 128)

    def copy(self, n, src, dst, to):
        rdma(src, dst, self.ss.at[n], self.rs.at[n], to).start()

    @scoped("sum_start")
    def start(self):
        other = 1 - self.place.k
        self.copy(0, self.part.at[self.half(other)], self.kin, self.place.at(k=other))

    def half(self, k):
        rows = self.rows // 2
        return pl.ds(pl.multiple_of(k * rows, rows), rows)

    @scoped("sum_first")
    def scatter(self):
        pc = self.place
        pc.wait_recv(self.kin, self.rs.at[0])
        both = (self.part[self.half(pc.k), :].astype(F32) + self.kin[...].astype(F32)).astype(BF16)
        for i in range(4):
            for j in range(4):
                self.out[i, j] = both[self.spot(i, j)]
        if self.second is None:

            def send(d, _):
                x, y = pc.chip(d)
                self.copy(1, self.out.at[x, y], self.in_a.at[pc.q], pc.at(x=x, y=y))
                return _

            lax.fori_loop(1, 16, send, 0)
            self.in_a[pc.q] = self.out[self.a, self.b]
        else:
            for d in (1, 3, 2):
                c, to = pc.along(self.first, d)
                self.copy(1, self.out.at[c], self.in_a.at[pl.ds(4 * self.a, 4)], to)
            self.in_a[pl.ds(4 * self.a, 4)] = self.out[self.a]

    @scoped("sum_second")
    def scatter_second(self):
        pc = self.place
        pc.wait_recv(self.in_a.at[pl.ds(0, 12)], self.rs.at[1])
        self.mid[...] = sum(self.in_a[4 * i : 4 * i + 4].astype(F32) for i in range(4)).astype(BF16)
        for d in (1, 3, 2):
            c, to = pc.along(self.second, d)
            self.copy(2, self.mid.at[c], self.in_b.at[self.b], to)
        self.in_b[self.b] = self.mid[self.b]

    @scoped("sum_column")
    def column(self):
        pc = self.place
        if self.second is None:
            self.wait_15(pc.wait_recv, self.rs.at[1])
            total = jnp.sum(self.in_a[...].astype(F32), axis=0)
        else:
            pc.wait_recv(self.in_b.at[pl.ds(0, 3)], self.rs.at[2])
            total = jnp.sum(self.in_b[...].astype(F32), axis=0)
        self.zbuf[pc.z] = total.astype(BF16)

        def send(d, _):
            self.copy(3, self.zbuf.at[pc.z], self.zbuf.at[pc.z], pc.along("z", d)[1])
            return _

        lax.fori_loop(1, 8, send, 0)

    def wait_15(self, wait, sem):
        wait(self.in_a.at[pl.ds(0, 15)], sem)

    @scoped("sum_spread")
    def spread(self):
        pc = self.place
        pc.wait_recv(self.zbuf.at[pl.ds(0, 7)], self.rs.at[3])
        self.whole[pc.k, self.a, self.b] = (jnp.sum(self.zbuf[...].astype(F32), axis=0) * self.factor).astype(BF16)
        mine = self.whole.at[pc.k, self.a, self.b]
        if self.second is None:

            def send(d, _):
                x, y = pc.chip(d)
                self.copy(4, mine, mine, pc.at(x=x, y=y))
                return _

            lax.fori_loop(1, 16, send, 0)
        else:
            for d in (1, 3, 2):
                self.copy(4, mine, mine, pc.along(self.first if self.turn else self.second, d)[1])

    @scoped("sum_spread_first")
    def spread_first(self):
        pc = self.place
        pc.wait_recv(self.in_b.at[pl.ds(0, 3)], self.rs.at[4])
        mine = self.whole.at[pc.k, :, self.b] if self.turn else self.whole.at[pc.k, self.a]
        for d in (1, 3, 2):
            self.copy(5, mine, mine, pc.along(self.second if self.turn else self.first, d)[1])

    @scoped("sum_cross")
    def cross(self):
        pc = self.place
        if self.second is None:
            self.wait_15(pc.wait_recv, self.rs.at[4])
        else:
            pc.wait_recv(self.in_a.at[pl.ds(0, 12)], self.rs.at[5])
        mine = self.whole.at[pc.k]
        self.copy(6, mine, mine, pc.at(k=1 - pc.k))

    @scoped("sum_finish")
    def finish(self, out_ref, base):
        pc, half = self.place, self.rows // 2
        pc.wait_recv(self.whole.at[0], self.rs.at[6])
        for h in range(2):
            for i in range(4):
                for j in range(4):
                    rows, lanes = self.spot(i, j)
                    at = base + h * half
                    out_ref[at + rows.start : at + rows.stop, lanes] = self.whole[h, i, j]

    @scoped("sum_drain")
    def drain(self):
        pc = self.place
        pc.wait_send(self.kin, self.ss.at[0])
        pc.wait_send(self.zbuf.at[pl.ds(0, 7)], self.ss.at[3])
        pc.wait_send(self.whole.at[0], self.ss.at[6])
        if self.second is None:
            self.wait_15(pc.wait_send, self.ss.at[1])
            self.wait_15(pc.wait_send, self.ss.at[4])
        else:
            pc.wait_send(self.in_a.at[pl.ds(0, 12)], self.ss.at[1])
            pc.wait_send(self.in_b.at[pl.ds(0, 3)], self.ss.at[2])
            pc.wait_send(self.in_b.at[pl.ds(0, 3)], self.ss.at[4])
            pc.wait_send(self.in_a.at[pl.ds(0, 12)], self.ss.at[5])


def kernel(factor, *refs):
    nf_hbm, og_hbm, mask_hbm, deg_hbm, adj_ref, ws_hbm, wn_hbm = refs[:7]
    ig_ref, gs_ref, gn_ref = refs[7:10]
    (
        adj, wide_mask, feats, ws, wn, grad_t, ig_t, og_ref, mask_ref, deg_ref,
        local_sem, z_ss, z_rs, y_ss, near_rs, far_rs, k_ss, k_rs, f_ss, f_rs, b_ss, b_rs,
    ) = refs[10:32]
    gath, acc, part, rx, zout, zin, own = [refs[32 + i : 53 + i : 7] for i in range(7)]
    rest = refs[53:]
    pc = Place()
    all_self, early, late = [Total(pc, *spec, factor, rest[10 * i : 10 * i + 10]) for i, spec in enumerate(SUMS)]

    barrier = pltpu.get_barrier_semaphore()

    def hello(to):
        pl.semaphore_signal(barrier, inc=1, device_id=to, device_id_type=MESH)

    def hello_z(d, _):
        hello(pc.along("z", d)[1])
        return _

    def hello_plane(d, _):
        x, y = pc.chip(d)
        hello(pc.at(x=x, y=y))
        return _

    lax.fori_loop(1, 8, hello_z, 0)
    lax.fori_loop(1, 16, hello_plane, 0)
    hello(pc.at(k=1 - pc.k))

    def group(s):
        return jnp.bitwise_xor(pc.zl, s)

    def adj_copy(s):
        rows = pl.ds(pl.multiple_of(group(s) * 1024, 1024), 1024)
        return pltpu.make_async_copy(adj_ref.at[rows], adj.at[rows], local_sem.at[s])

    w_copies = [pltpu.make_async_copy(ws_hbm, ws, local_sem.at[4]), pltpu.make_async_copy(wn_hbm, wn, local_sem.at[5])]
    small = [(og_hbm, og_ref), (deg_hbm, deg_ref), (nf_hbm, feats.at[pc.row]), (mask_hbm, mask_ref)]
    in_copies = [pltpu.make_async_copy(src, dst, local_sem.at[6 + i]) for i, (src, dst) in enumerate(small)]
    for copy in in_copies:
        copy.start()
    for s in range(4):
        adj_copy(s).start()
    for copy in w_copies:
        copy.start()
    in_copies[0].wait()
    in_copies[1].wait()

    turned = og_ref[...].astype(F32).T
    grad_t[...] = turned.astype(BF16)
    scaled_t = (turned / deg_ref[...].astype(F32)).astype(BF16)
    for ch in range(PARTS):
        gath[ch][pc.zl, pc.k, pc.y] = scaled_t[STARTS[ch] : STARTS[ch] + SIZES[ch]]

    def spread_mask():
        in_copies[3].wait()
        lane_tile = lax.div(lax.broadcasted_iota(jnp.int32, (8, 1024), 1), 128)
        pick = (lane_tile == lax.broadcasted_iota(jnp.int32, (8, 1024), 0)).astype(F32).astype(BF16)
        wide_mask[...] = jnp.dot(mask_ref[...].astype(F32).T.astype(BF16), pick, preferred_element_type=F32)

    def own_sum():
        all_self.part[...] = jnp.dot(grad_t[...], feats[pc.row], preferred_element_type=F32).astype(BF16)

    @scoped("apply_mask")
    def apply_mask(s):
        adj_copy(s).wait()

        def tile(t, _):
            row = group(s) * 8 + t
            rows = pl.ds(pl.multiple_of(row * 128, 128), 128)
            adj[rows, :] = adj[rows, :] * wide_mask[pl.ds(row, 1), :].astype(BF16)
            return _

        lax.fori_loop(0, 8, tile, 0)

    with jax.named_scope("greeting"):
        pl.semaphore_wait(barrier, 23)


    up, up_to = pc.along("y", 1)
    down, down_to = pc.along("y", 3)
    far_y = lax.rem(pc.y + 2, 4)

    def near(ch, s):
        block = gath[ch].at[group(s), pc.k, pc.y]
        for d in (1, 3, 2):
            rdma(block, block, y_ss, near_rs.at[ch, s], pc.along("y", d)[1]).start()

    @scoped("stage_near")
    def stage_near(ch, s):
        if s > 0:
            pc.wait_recv(gath[ch].at[group(s), pc.k, pc.y], z_rs.at[ch, s])
            near(ch, s)

    def stage_far(ch, s):
        pass

    @scoped("stage_core")
    def stage_core(ch, s):
        pc.wait_recv(gath[ch].at[group(s), pc.k, pl.ds(0, 3)], near_rs.at[ch, s])
        mine = gath[ch].at[group(s), pc.k]
        rdma(mine, mine, k_ss, k_rs.at[ch, s], pc.at(k=1 - pc.k)).start()

    @scoped("multiply")
    def multiply(ch, s):
        g = group(s)
        pc.wait_recv(gath[ch].at[g, 1 - pc.k], k_rs.at[ch, s])
        with jax.named_scope("dot"):
            rows = pl.ds(pl.multiple_of(g * 1024, 1024), 1024)
            left = jnp.concatenate([gath[ch][g, k, y] for y in range(4) for k in range(2)], axis=1)

            term = jnp.dot(left, adj[rows, :], preferred_element_type=F32)
            acc[ch][...] = term if s == 0 else acc[ch][...] + term

    items = [(ch, 0) for ch in range(PARTS)] + [(ch, s) for ch in range(PARTS) for s in range(1, 4)]

    @scoped("z_sends")
    def z_sends(ch):
        mine = gath[ch].at[pc.zl, pc.k, pc.y]
        for s in range(1, 4):
            rdma(mine, mine, z_ss, z_rs.at[ch, s], pc.at(z=pc.zh * 4 + group(s))).start()

    far_row = (1 - pc.zh) * 4 + pc.x
    right, right_to = pc.along("x", 1)
    left_x, left_to = pc.along("x", 3)

    @scoped("feats")
    def feats_near(n, row):
        block = feats.at[row]
        rdma(block, block, f_ss, f_rs.at[n], right_to).start()
        rdma(block, block, f_ss, f_rs.at[n], left_to).start()

    @scoped("feats")
    def feats_far(n, zh):
        pc.wait_recv(feats.at[pl.ds(0, 2)], f_rs.at[n])
        low = feats.at[zh * 4 + left_x, pl.ds(0, HALF)]
        high = feats.at[zh * 4 + right, pl.ds(HALF, HALF)]
        rdma(low, low, f_ss, f_rs.at[n + 1], right_to).start()
        rdma(high, high, f_ss, f_rs.at[n + 1], left_to).start()

    @scoped("send_rows")
    def send_rows(ch):
        for r in range(8):
            part[ch][r % 4, r // 4] = acc[ch][:, r * 128 : (r + 1) * 128].astype(BF16)

    @scoped("rows_x_start")
    def rows_x_start(ch):
        for d in (1, 3, 2):
            x, to = pc.along("x", d)
            rdma(part[ch].at[x], rx[ch].at[d - 1], b_ss.at[ch, 0], b_rs.at[ch, 0], to).start()

    @scoped("neigh")
    def neigh(ch):
        left = jnp.concatenate([part[ch][r % 4, r // 4] for r in range(8)], axis=1)
        value = jnp.dot(left, feats[...].reshape(8 * NODE, FEAT), preferred_element_type=F32)
        if ch < 2:
            early.part[STARTS[ch] : STARTS[ch] + SIZES[ch]] = value.astype(BF16)
        else:
            late.part[...] = value.astype(BF16)
        if ch > 0:
            (early if ch == 1 else late).start()

    @scoped("rows_over_x")
    def rows_over_x(ch):
        pc.wait_recv(rx[ch], b_rs.at[ch, 0])

        def total(zh):
            terms = [part[ch][pc.x, zh]] + [rx[ch][d, zh] for d in range(3)]
            return sum(t.astype(F32) for t in terms)

        zout[ch][...] = total(1 - pc.zh).astype(BF16)
        rdma(zout[ch], zin[ch], b_ss.at[ch, 1], b_rs.at[ch, 1], pc.along("z", 4)[1]).start()
        own[ch][...] = total(pc.zh)

    @scoped("rows_over_z")
    def rows_over_z(ch):
        pc.wait_recv(zin[ch], b_rs.at[ch, 1])
        pulled = (own[ch][...] + zin[ch][...].astype(F32)).astype(BF16)
        ig_t[...] += jnp.dot(wn[:, STARTS[ch] : STARTS[ch] + SIZES[ch]], pulled, preferred_element_type=F32)

    @scoped("own_term")
    def own_term():
        for copy in w_copies:
            copy.wait()
        ig_t[...] = jnp.dot(ws[...], grad_t[...], preferred_element_type=F32)

    def to_far_z():
        mine = feats.at[pc.row]
        rdma(mine, mine, f_ss, f_rs.at[0], pc.along("z", 4)[1]).start()

    def from_far_z():
        pc.wait_recv(feats.at[far_row], f_rs.at[0])
        feats_near(3, far_row)

    def feats_wait():
        pc.wait_recv(feats.at[0], f_rs.at[2])
        pc.wait_recv(feats.at[0], f_rs.at[4])

    def close(ch):
        send_rows(ch)
        neigh(ch)

    def far(i):
        stage_far(*items[i])

    def forward(i):
        stage_near(*items[i])

    def core(i):
        stage_core(*items[i])

    def dot(i):
        multiply(*items[i])

    near(0, 0)
    z_sends(0)
    in_copies[2].wait()
    own_sum()
    all_self.start()
    spread_mask()
    apply_mask(0)
    near(1, 0)
    near(2, 0)
    feats_near(1, pc.row)
    apply_mask(1)
    apply_mask(2)
    forward(3)
    core(0)
    forward(4)
    core(1)
    core(2)
    forward(5)
    to_far_z()
    z_sends(1)
    z_sends(2)
    dot(0)
    all_self.scatter()
    core(3)
    dot(1)
    feats_far(1, pc.zh)
    core(4)
    dot(2)
    apply_mask(3)
    dot(3)
    core(5)
    from_far_z()
    forward(6)
    all_self.scatter_second()
    dot(4)
    forward(7)
    forward(8)
    own_term()
    dot(5)
    forward(9)
    forward(10)
    core(6)
    send_rows(0)
    feats_far(3, 1 - pc.zh)
    rows_x_start(0)
    forward(11)
    core(7)
    all_self.column()
    core(8)
    dot(6)
    core(9)
    dot(7)
    feats_wait()
    neigh(0)
    core(10)
    dot(8)
    send_rows(1)
    neigh(1)
    core(11)
    all_self.spread()
    dot(9)
    early.scatter()
    dot(10)
    dot(11)
    send_rows(2)
    neigh(2)
    rows_over_x(0)
    late.scatter()
    rows_x_start(1)
    early.column()
    rows_x_start(2)
    rows_over_z(0)
    late.column()
    all_self.spread_first()
    early.spread()
    rows_over_x(1)
    late.spread()
    rows_over_x(2)
    early.cross()
    all_self.cross()
    rows_over_z(1)
    late.cross()
    all_self.finish(gs_ref, 0)
    early.finish(gn_ref, 0)
    rows_over_z(2)
    ig_ref[...] = ig_t[...].T.astype(BF16)
    late.finish(gn_ref, STARTS[2])

    with jax.named_scope("drain"):
        for blocks in gath:
            pc.wait_send(blocks.at[pl.ds(0, 3), 0, 0], z_ss)
            pc.wait_send(blocks.at[pl.ds(0, 3), 0], y_ss)
            pc.wait_send(blocks.at[:, 0], k_ss)
        pc.wait_send(feats.at[pl.ds(0, 7)], f_ss)
        for ch in range(PARTS):
            pc.wait_send(rx[ch], b_ss.at[ch, 0])
            pc.wait_send(zin[ch], b_ss.at[ch, 1])
        for total in (all_self, early, late):
            total.drain()


def finish_kernel(ig_ref, gs_ref, gn_ref, ig_out, gs_out, gn_out):
    ig_out[...] = ig_ref[...]
    gs_out[...] = gs_ref[...].astype(F32).T
    gn_out[...] = gn_ref[...].astype(F32).T


def local(node_features, out_grad, adjacency, tile_mask, degrees, w_self, w_neigh):
    node_count = NODE * lax.axis_size("row") * lax.axis_size("col")
    factor = 1.0 / math.sqrt(node_count)
    vmem = pl.BlockSpec(memory_space=pltpu.VMEM)
    hbm = pl.BlockSpec(memory_space=pl.ANY)
    dma = pltpu.SemaphoreType.DMA
    scratch = [
        pltpu.VMEM((4096, 1024), BF16),
        pltpu.VMEM((32, 1024), F32),
        pltpu.VMEM((8, NODE, FEAT), BF16),
        pltpu.VMEM((FEAT, FEAT), BF16),
        pltpu.VMEM((FEAT, FEAT), BF16),
        pltpu.VMEM((FEAT, NODE), BF16),
        pltpu.VMEM((FEAT, NODE), F32),
        pltpu.VMEM((NODE, FEAT), BF16),
        pltpu.VMEM((8, 32), jnp.int32),
        pltpu.VMEM((1, NODE), jnp.int32),
        dma((10,)),
        dma,
        dma((PARTS, 4)),
        dma,
        dma((PARTS, 4)),
        dma((PARTS, 4)),
        dma,
        dma((PARTS, 4)),
        dma,
        dma((5,)),
        dma((PARTS, 2)),
        dma((PARTS, 2)),
    ]
    for size in SIZES:
        scratch += [
            pltpu.VMEM((4, 2, 4, size, NODE), BF16),
            pltpu.VMEM((size, 1024), F32),
            pltpu.VMEM((4, 2, size, NODE), BF16),
            pltpu.VMEM((3, 2, size, NODE), BF16),
            pltpu.VMEM((size, NODE), BF16),
            pltpu.VMEM((size, NODE), BF16),
            pltpu.VMEM((size, NODE), F32),
        ]
    for rows, _, _, _ in SUMS:
        scratch += Total.scratch(rows)
    shapes = [pltpu.VMEM((n, FEAT), BF16) for n in (NODE, FEAT, FEAT)]
    results = pl.pallas_call(
        lambda *refs: kernel(factor, *refs),
        out_shape=shapes,
        in_specs=[hbm] * 7,
        out_specs=(vmem, vmem, vmem),
        scratch_shapes=scratch,
        compiler_params=pltpu.CompilerParams(
            collective_id=0, has_side_effects=True, vmem_limit_bytes=56 * 1024 * 1024
        ),
    )(node_features, out_grad, tile_mask.T, degrees.reshape(1, NODE), adjacency, w_self, w_neigh)
    return pl.pallas_call(
        finish_kernel,
        out_shape=[jax.ShapeDtypeStruct((n, FEAT), t) for n, t in ((NODE, BF16), (FEAT, F32), (FEAT, F32))],
        in_specs=[vmem] * 3,
        out_specs=[vmem] * 3,
        compiler_params=pltpu.CompilerParams(vmem_limit_bytes=16 * 1024 * 1024),
    )(*results)


def solution(mesh):
    in_specs = (
        P(("row", "col"), None),
        P(("row", "col"), None),
        P("row", "col"),
        P("row", "col"),
        P(("row", "col")),
        P(),
        P(),
    )
    out_specs = (P(("row", "col"), None), P(), P())
    return jax.shard_map(local, mesh=mesh, in_specs=in_specs, out_specs=out_specs, check_vma=False)
```

```python
import math

import jax
import jax.numpy as jnp
from jax import lax
from jax.experimental import pallas as pl
from jax.experimental.pallas import tpu as pltpu
from jax.sharding import PartitionSpec as P

MESH = pl.DeviceIdType.MESH
F32, BF16 = jnp.float32, jnp.bfloat16
FEAT = 512
NODE = 128
SIZES = (256, 128, 128)
STARTS = (0, 256, 384)
PARTS = 3
HALF = NODE // 2
SUMS = ((512, "x", "y", True), (384, "xy", None, False), (128, "xy", None, False))


def scoped(name):
    def wrap(fn):
        def call(*args):
            with jax.named_scope(name):
                return fn(*args)

        return call

    return wrap


def rdma(src, dst, send_sem, recv_sem, to):
    return pltpu.make_async_remote_copy(
        src_ref=src, dst_ref=dst, send_sem=send_sem, recv_sem=recv_sem, device_id=to, device_id_type=MESH
    )


class Place:
    def __init__(self):
        row, col = lax.axis_index("row"), lax.axis_index("col")
        self.row, self.col = row, col
        self.x, self.zh = lax.rem(row, 4), lax.div(row, 4)
        self.zl, self.y, self.k = lax.div(col, 8), lax.rem(lax.div(col, 2), 4), lax.rem(col, 2)
        self.z = self.zh * 4 + self.zl
        self.q = self.x * 4 + self.y

    def at(self, x=None, y=None, z=None, k=None):
        x = self.x if x is None else x
        y = self.y if y is None else y
        z = self.z if z is None else z
        k = self.k if k is None else k
        return (lax.div(z, 4) * 4 + x, lax.rem(z, 4) * 8 + y * 2 + k)

    def chip(self, d):
        q = lax.rem(self.q + d, 16)
        return lax.div(q, 4), lax.rem(q, 4)

    def along(self, axis, d):
        size = 8 if axis == "z" else 4
        c = lax.rem(getattr(self, axis) + d, size)
        return c, self.at(**{axis: c})

    def wait_recv(self, ref, sem):
        rdma(ref, ref, sem, sem, self.at()).wait_recv()

    def wait_send(self, ref, sem):
        rdma(ref, ref, sem, sem, self.at()).wait_send()


class Total:
    def __init__(self, place, rows, first, second, turn, factor, refs):
        self.place, self.rows, self.first, self.second, self.turn, self.factor = place, rows, first, second, turn, factor
        self.part, self.kin, self.out, self.in_a, self.mid, self.in_b, self.zbuf, self.whole, self.ss, self.rs = refs
        if second is None:
            self.a, self.b = place.x, place.y
        else:
            self.a, self.b = getattr(place, first), getattr(place, second)

    @staticmethod
    def scratch(rows):
        piece = (rows // 8, 128)
        return [
            pltpu.VMEM((rows, FEAT), BF16),
            pltpu.VMEM((rows // 2, FEAT), BF16),
            pltpu.VMEM((4, 4) + piece, BF16),
            pltpu.VMEM((16,) + piece, BF16),
            pltpu.VMEM((4,) + piece, BF16),
            pltpu.VMEM((4,) + piece, BF16),
            pltpu.VMEM((8,) + piece, BF16),
            pltpu.VMEM((2, 4, 4) + piece, BF16),
            pltpu.SemaphoreType.DMA((7,)),
            pltpu.SemaphoreType.DMA((7,)),
        ]

    def spot(self, i, j):
        tall = self.rows // 8
        return slice(i * tall, (i + 1) * tall), slice(j * 128, (j + 1) * 128)

    def copy(self, n, src, dst, to):
        rdma(src, dst, self.ss.at[n], self.rs.at[n], to).start()

    @scoped("sum_start")
    def start(self):
        other = 1 - self.place.k
        self.copy(0, self.part.at[self.half(other)], self.kin, self.place.at(k=other))

    def half(self, k):
        rows = self.rows // 2
        return pl.ds(pl.multiple_of(k * rows, rows), rows)

    @scoped("sum_first")
    def scatter(self):
        pc = self.place
        pc.wait_recv(self.kin, self.rs.at[0])
        both = (self.part[self.half(pc.k), :].astype(F32) + self.kin[...].astype(F32)).astype(BF16)
        for i in range(4):
            for j in range(4):
                self.out[i, j] = both[self.spot(i, j)]
        if self.second is None:

            def send(d, _):
                x, y = pc.chip(lax.rem(d + 8, 15) + 1)
                self.copy(1, self.out.at[x, y], self.in_a.at[pc.q], pc.at(x=x, y=y))
                return _

            lax.fori_loop(1, 16, send, 0)
            self.in_a[pc.q] = self.out[self.a, self.b]
        else:
            for d in (1, 3, 2):
                c, to = pc.along(self.first, d)
                self.copy(1, self.out.at[c], self.in_a.at[pl.ds(4 * self.a, 4)], to)
            self.in_a[pl.ds(4 * self.a, 4)] = self.out[self.a]

    @scoped("sum_second")
    def scatter_second(self):
        pc = self.place
        pc.wait_recv(self.in_a.at[pl.ds(0, 12)], self.rs.at[1])
        self.mid[...] = sum(self.in_a[4 * i : 4 * i + 4].astype(F32) for i in range(4)).astype(BF16)
        for d in (1, 3, 2):
            c, to = pc.along(self.second, d)
            self.copy(2, self.mid.at[c], self.in_b.at[self.b], to)
        self.in_b[self.b] = self.mid[self.b]

    @scoped("sum_column")
    def column(self):
        pc = self.place
        if self.second is None:
            self.wait_15(pc.wait_recv, self.rs.at[1])
            total = jnp.sum(self.in_a[...].astype(F32), axis=0)
        else:
            pc.wait_recv(self.in_b.at[pl.ds(0, 3)], self.rs.at[2])
            total = jnp.sum(self.in_b[...].astype(F32), axis=0)
        self.zbuf[pc.z] = total.astype(BF16)

        def send(d, _):
            self.copy(3, self.zbuf.at[pc.z], self.zbuf.at[pc.z], pc.along("z", lax.rem(d + 2, 7) + 1)[1])
            return _

        lax.fori_loop(1, 8, send, 0)

    def wait_15(self, wait, sem):
        wait(self.in_a.at[pl.ds(0, 15)], sem)

    @scoped("sum_spread")
    def spread(self):
        pc = self.place
        pc.wait_recv(self.zbuf.at[pl.ds(0, 7)], self.rs.at[3])
        self.whole[pc.k, self.a, self.b] = (jnp.sum(self.zbuf[...].astype(F32), axis=0) * self.factor).astype(BF16)
        mine = self.whole.at[pc.k, self.a, self.b]
        if self.second is None:

            def send(d, _):
                x, y = pc.chip(lax.rem(d + 8, 15) + 1)
                self.copy(4, mine, mine, pc.at(x=x, y=y))
                return _

            lax.fori_loop(1, 16, send, 0)
        else:
            for d in (1, 3, 2):
                self.copy(4, mine, mine, pc.along(self.first if self.turn else self.second, d)[1])

    @scoped("sum_spread_first")
    def spread_first(self):
        pc = self.place
        pc.wait_recv(self.in_b.at[pl.ds(0, 3)], self.rs.at[4])
        mine = self.whole.at[pc.k, :, self.b] if self.turn else self.whole.at[pc.k, self.a]
        for d in (1, 3, 2):
            self.copy(5, mine, mine, pc.along(self.second if self.turn else self.first, d)[1])

    @scoped("sum_cross")
    def cross(self):
        pc = self.place
        if self.second is None:
            self.wait_15(pc.wait_recv, self.rs.at[4])
        else:
            pc.wait_recv(self.in_a.at[pl.ds(0, 12)], self.rs.at[5])
        mine = self.whole.at[pc.k]
        self.copy(6, mine, mine, pc.at(k=1 - pc.k))

    @scoped("sum_finish")
    def finish(self, out_ref, base):
        pc, half = self.place, self.rows // 2
        pc.wait_recv(self.whole.at[0], self.rs.at[6])
        for h in range(2):
            for i in range(4):
                for j in range(4):
                    rows, lanes = self.spot(i, j)
                    at = base + h * half
                    out_ref[at + rows.start : at + rows.stop, lanes] = self.whole[h, i, j]

    @scoped("sum_drain")
    def drain(self):
        pc = self.place
        pc.wait_send(self.kin, self.ss.at[0])
        pc.wait_send(self.zbuf.at[pl.ds(0, 7)], self.ss.at[3])
        pc.wait_send(self.whole.at[0], self.ss.at[6])
        if self.second is None:
            self.wait_15(pc.wait_send, self.ss.at[1])
            self.wait_15(pc.wait_send, self.ss.at[4])
        else:
            pc.wait_send(self.in_a.at[pl.ds(0, 12)], self.ss.at[1])
            pc.wait_send(self.in_b.at[pl.ds(0, 3)], self.ss.at[2])
            pc.wait_send(self.in_b.at[pl.ds(0, 3)], self.ss.at[4])
            pc.wait_send(self.in_a.at[pl.ds(0, 12)], self.ss.at[5])


def kernel(factor, *refs):
    nf_hbm, og_hbm, mask_hbm, deg_hbm, adj_ref, ws_hbm, wn_hbm = refs[:7]
    ig_ref, gs_ref, gn_ref = refs[7:10]
    (
        adj, wide_mask, feats, ws, wn, grad_t, ig_t, og_ref, mask_ref, deg_ref,
        local_sem, z_ss, z_rs, y_ss, near_rs, far_rs, k_ss, k_rs, f_ss, f_rs, b_ss, b_rs,
    ) = refs[10:32]
    gath, acc, part, rx, zout, zin, own = [refs[32 + i : 53 + i : 7] for i in range(7)]
    rest = refs[53:]
    pc = Place()
    all_self, early, late = [Total(pc, *spec, factor, rest[10 * i : 10 * i + 10]) for i, spec in enumerate(SUMS)]

    barrier = pltpu.get_barrier_semaphore()

    def hello(to):
        pl.semaphore_signal(barrier, inc=1, device_id=to, device_id_type=MESH)

    def hello_z(d, _):
        hello(pc.along("z", d)[1])
        return _

    def hello_plane(d, _):
        x, y = pc.chip(d)
        hello(pc.at(x=x, y=y))
        return _

    lax.fori_loop(1, 8, hello_z, 0)
    lax.fori_loop(1, 16, hello_plane, 0)
    hello(pc.at(k=1 - pc.k))

    def group(s):
        return jnp.bitwise_xor(pc.zl, s)

    def adj_copy(s):
        rows = pl.ds(pl.multiple_of(group(s) * 1024, 1024), 1024)
        return pltpu.make_async_copy(adj_ref.at[rows], adj.at[rows], local_sem.at[s])

    w_copies = [pltpu.make_async_copy(ws_hbm, ws, local_sem.at[4]), pltpu.make_async_copy(wn_hbm, wn, local_sem.at[5])]
    small = [(og_hbm, og_ref), (deg_hbm, deg_ref), (nf_hbm, feats.at[pc.row]), (mask_hbm, mask_ref)]
    in_copies = [pltpu.make_async_copy(src, dst, local_sem.at[6 + i]) for i, (src, dst) in enumerate(small)]
    for copy in in_copies:
        copy.start()
    for s in range(4):
        adj_copy(s).start()
    for copy in w_copies:
        copy.start()
    in_copies[0].wait()
    in_copies[1].wait()

    turned = og_ref[...].astype(F32).T
    grad_t[...] = turned.astype(BF16)
    scaled_t = (turned / deg_ref[...].astype(F32)).astype(BF16)
    for ch in range(PARTS):
        gath[ch][pc.zl, pc.k, pc.y] = scaled_t[STARTS[ch] : STARTS[ch] + SIZES[ch]]

    def spread_mask():
        in_copies[3].wait()
        lane_tile = lax.div(lax.broadcasted_iota(jnp.int32, (8, 1024), 1), 128)
        pick = (lane_tile == lax.broadcasted_iota(jnp.int32, (8, 1024), 0)).astype(F32).astype(BF16)
        wide_mask[...] = jnp.dot(mask_ref[...].astype(F32).T.astype(BF16), pick, preferred_element_type=F32)

    def own_sum():
        all_self.part[...] = jnp.dot(grad_t[...], feats[pc.row], preferred_element_type=F32).astype(BF16)

    @scoped("apply_mask")
    def apply_mask(s):
        adj_copy(s).wait()

        def tile(t, _):
            row = group(s) * 8 + t
            rows = pl.ds(pl.multiple_of(row * 128, 128), 128)
            adj[rows, :] = adj[rows, :] * wide_mask[pl.ds(row, 1), :].astype(BF16)
            return _

        lax.fori_loop(0, 8, tile, 0)

    with jax.named_scope("greeting"):
        pl.semaphore_wait(barrier, 23)


    up, up_to = pc.along("y", 1)
    down, down_to = pc.along("y", 3)
    far_y = lax.rem(pc.y + 2, 4)

    def near(ch, s):
        block = gath[ch].at[group(s), pc.k, pc.y]
        for d in (1, 3, 2):
            rdma(block, block, y_ss, near_rs.at[ch, s], pc.along("y", d)[1]).start()

    @scoped("stage_near")
    def stage_near(ch, s):
        if s > 0:
            pc.wait_recv(gath[ch].at[group(s), pc.k, pc.y], z_rs.at[ch, s])
            near(ch, s)

    def stage_far(ch, s):
        pass

    @scoped("stage_core")
    def stage_core(ch, s):
        pc.wait_recv(gath[ch].at[group(s), pc.k, pl.ds(0, 3)], near_rs.at[ch, s])
        mine = gath[ch].at[group(s), pc.k]
        rdma(mine, mine, k_ss, k_rs.at[ch, s], pc.at(k=1 - pc.k)).start()

    @scoped("multiply")
    def multiply(ch, s):
        g = group(s)
        pc.wait_recv(gath[ch].at[g, 1 - pc.k], k_rs.at[ch, s])
        with jax.named_scope("dot"):
            rows = pl.ds(pl.multiple_of(g * 1024, 1024), 1024)
            left = jnp.concatenate([gath[ch][g, k, y] for y in range(4) for k in range(2)], axis=1)

            term = jnp.dot(left, adj[rows, :], preferred_element_type=F32)
            acc[ch][...] = term if s == 0 else acc[ch][...] + term

    items = [(ch, 0) for ch in range(PARTS)] + [(ch, s) for ch in range(PARTS) for s in range(1, 4)]

    @scoped("z_sends")
    def z_sends(ch):
        mine = gath[ch].at[pc.zl, pc.k, pc.y]
        for s in range(1, 4):
            rdma(mine, mine, z_ss, z_rs.at[ch, s], pc.at(z=pc.zh * 4 + group(s))).start()

    far_row = (1 - pc.zh) * 4 + pc.x
    right, right_to = pc.along("x", 1)
    left_x, left_to = pc.along("x", 3)

    @scoped("feats")
    def feats_near(n, row):
        block = feats.at[row]
        rdma(block, block, f_ss, f_rs.at[n], right_to).start()
        rdma(block, block, f_ss, f_rs.at[n], left_to).start()

    @scoped("feats")
    def feats_far(n, zh):
        pc.wait_recv(feats.at[pl.ds(0, 2)], f_rs.at[n])
        low = feats.at[zh * 4 + left_x, pl.ds(0, HALF)]
        high = feats.at[zh * 4 + right, pl.ds(HALF, HALF)]
        rdma(low, low, f_ss, f_rs.at[n + 1], right_to).start()
        rdma(high, high, f_ss, f_rs.at[n + 1], left_to).start()

    @scoped("send_rows")
    def send_rows(ch):
        for r in range(8):
            part[ch][r % 4, r // 4] = acc[ch][:, r * 128 : (r + 1) * 128].astype(BF16)

    @scoped("rows_x_start")
    def rows_x_start(ch):
        for d in (1, 3, 2):
            x, to = pc.along("x", d)
            rdma(part[ch].at[x], rx[ch].at[d - 1], b_ss.at[ch, 0], b_rs.at[ch, 0], to).start()

    @scoped("neigh")
    def neigh(ch):
        left = jnp.concatenate([part[ch][r % 4, r // 4] for r in range(8)], axis=1)
        value = jnp.dot(left, feats[...].reshape(8 * NODE, FEAT), preferred_element_type=F32)
        if ch < 2:
            early.part[STARTS[ch] : STARTS[ch] + SIZES[ch]] = value.astype(BF16)
        else:
            late.part[...] = value.astype(BF16)
        if ch > 0:
            (early if ch == 1 else late).start()

    @scoped("rows_over_x")
    def rows_over_x(ch):
        pc.wait_recv(rx[ch], b_rs.at[ch, 0])

        def total(zh):
            terms = [part[ch][pc.x, zh]] + [rx[ch][d, zh] for d in range(3)]
            return sum(t.astype(F32) for t in terms)

        zout[ch][...] = total(1 - pc.zh).astype(BF16)
        rdma(zout[ch], zin[ch], b_ss.at[ch, 1], b_rs.at[ch, 1], pc.along("z", 4)[1]).start()
        own[ch][...] = total(pc.zh)

    @scoped("rows_over_z")
    def rows_over_z(ch):
        pc.wait_recv(zin[ch], b_rs.at[ch, 1])
        pulled = (own[ch][...] + zin[ch][...].astype(F32)).astype(BF16)
        ig_t[...] += jnp.dot(wn[:, STARTS[ch] : STARTS[ch] + SIZES[ch]], pulled, preferred_element_type=F32)

    @scoped("own_term")
    def own_term():
        for copy in w_copies:
            copy.wait()
        ig_t[...] = jnp.dot(ws[...], grad_t[...], preferred_element_type=F32)

    def to_far_z():
        mine = feats.at[pc.row]
        rdma(mine, mine, f_ss, f_rs.at[0], pc.along("z", 4)[1]).start()

    def from_far_z():
        pc.wait_recv(feats.at[far_row], f_rs.at[0])
        feats_near(3, far_row)

    def feats_wait():
        pc.wait_recv(feats.at[0], f_rs.at[2])
        pc.wait_recv(feats.at[0], f_rs.at[4])

    def close(ch):
        send_rows(ch)
        neigh(ch)

    def far(i):
        stage_far(*items[i])

    def forward(i):
        stage_near(*items[i])

    def core(i):
        stage_core(*items[i])

    def dot(i):
        multiply(*items[i])

    near(0, 0)
    z_sends(0)
    in_copies[2].wait()
    own_sum()
    all_self.start()
    spread_mask()
    apply_mask(0)
    near(1, 0)
    near(2, 0)
    feats_near(1, pc.row)
    apply_mask(1)
    apply_mask(2)
    forward(3)
    core(0)
    forward(4)
    core(1)
    core(2)
    forward(5)
    to_far_z()
    z_sends(1)
    z_sends(2)
    dot(0)
    all_self.scatter()
    core(3)
    dot(1)
    feats_far(1, pc.zh)
    core(4)
    dot(2)
    apply_mask(3)
    dot(3)
    core(5)
    from_far_z()
    forward(6)
    all_self.scatter_second()
    dot(4)
    forward(7)
    forward(8)
    own_term()
    dot(5)
    forward(9)
    forward(10)
    core(6)
    send_rows(0)
    feats_far(3, 1 - pc.zh)
    rows_x_start(0)
    forward(11)
    core(7)
    all_self.column()
    core(8)
    dot(6)
    core(9)
    dot(7)
    feats_wait()
    neigh(0)
    core(10)
    dot(8)
    send_rows(1)
    neigh(1)
    core(11)
    all_self.spread()
    dot(9)
    early.scatter()
    dot(10)
    dot(11)
    send_rows(2)
    neigh(2)
    rows_over_x(0)
    late.scatter()
    rows_x_start(1)
    early.column()
    rows_x_start(2)
    rows_over_z(0)
    late.column()
    all_self.spread_first()
    early.spread()
    rows_over_x(1)
    late.spread()
    rows_over_x(2)
    early.cross()
    all_self.cross()
    rows_over_z(1)
    late.cross()
    all_self.finish(gs_ref, 0)
    early.finish(gn_ref, 0)
    rows_over_z(2)
    ig_ref[...] = ig_t[...].T.astype(BF16)
    late.finish(gn_ref, STARTS[2])

    with jax.named_scope("drain"):
        for blocks in gath:
            pc.wait_send(blocks.at[pl.ds(0, 3), 0, 0], z_ss)
            pc.wait_send(blocks.at[pl.ds(0, 3), 0], y_ss)
            pc.wait_send(blocks.at[:, 0], k_ss)
        pc.wait_send(feats.at[pl.ds(0, 7)], f_ss)
        for ch in range(PARTS):
            pc.wait_send(rx[ch], b_ss.at[ch, 0])
            pc.wait_send(zin[ch], b_ss.at[ch, 1])
        for total in (all_self, early, late):
            total.drain()


def finish_kernel(ig_ref, gs_ref, gn_ref, ig_out, gs_out, gn_out):
    ig_out[...] = ig_ref[...]
    gs_out[...] = gs_ref[...].astype(F32).T
    gn_out[...] = gn_ref[...].astype(F32).T


def local(node_features, out_grad, adjacency, tile_mask, degrees, w_self, w_neigh):
    node_count = NODE * lax.axis_size("row") * lax.axis_size("col")
    factor = 1.0 / math.sqrt(node_count)
    vmem = pl.BlockSpec(memory_space=pltpu.VMEM)
    hbm = pl.BlockSpec(memory_space=pl.ANY)
    dma = pltpu.SemaphoreType.DMA
    scratch = [
        pltpu.VMEM((4096, 1024), BF16),
        pltpu.VMEM((32, 1024), F32),
        pltpu.VMEM((8, NODE, FEAT), BF16),
        pltpu.VMEM((FEAT, FEAT), BF16),
        pltpu.VMEM((FEAT, FEAT), BF16),
        pltpu.VMEM((FEAT, NODE), BF16),
        pltpu.VMEM((FEAT, NODE), F32),
        pltpu.VMEM((NODE, FEAT), BF16),
        pltpu.VMEM((8, 32), jnp.int32),
        pltpu.VMEM((1, NODE), jnp.int32),
        dma((10,)),
        dma,
        dma((PARTS, 4)),
        dma,
        dma((PARTS, 4)),
        dma((PARTS, 4)),
        dma,
        dma((PARTS, 4)),
        dma,
        dma((5,)),
        dma((PARTS, 2)),
        dma((PARTS, 2)),
    ]
    for size in SIZES:
        scratch += [
            pltpu.VMEM((4, 2, 4, size, NODE), BF16),
            pltpu.VMEM((size, 1024), F32),
            pltpu.VMEM((4, 2, size, NODE), BF16),
            pltpu.VMEM((3, 2, size, NODE), BF16),
            pltpu.VMEM((size, NODE), BF16),
            pltpu.VMEM((size, NODE), BF16),
            pltpu.VMEM((size, NODE), F32),
        ]
    for rows, _, _, _ in SUMS:
        scratch += Total.scratch(rows)
    shapes = [pltpu.VMEM((n, FEAT), BF16) for n in (NODE, FEAT, FEAT)]
    results = pl.pallas_call(
        lambda *refs: kernel(factor, *refs),
        out_shape=shapes,
        in_specs=[hbm] * 7,
        out_specs=(vmem, vmem, vmem),
        scratch_shapes=scratch,
        compiler_params=pltpu.CompilerParams(
            collective_id=0, has_side_effects=True, vmem_limit_bytes=56 * 1024 * 1024
        ),
    )(node_features, out_grad, tile_mask.T, degrees.reshape(1, NODE), adjacency, w_self, w_neigh)
    return pl.pallas_call(
        finish_kernel,
        out_shape=[jax.ShapeDtypeStruct((n, FEAT), t) for n, t in ((NODE, BF16), (FEAT, F32), (FEAT, F32))],
        in_specs=[vmem] * 3,
        out_specs=[vmem] * 3,
        compiler_params=pltpu.CompilerParams(vmem_limit_bytes=16 * 1024 * 1024),
    )(*results)


def solution(mesh):
    in_specs = (
        P(("row", "col"), None),
        P(("row", "col"), None),
        P("row", "col"),
        P("row", "col"),
        P(("row", "col")),
        P(),
        P(),
    )
    out_specs = (P(("row", "col"), None), P(), P())
    return jax.shard_map(local, mesh=mesh, in_specs=in_specs, out_specs=out_specs, check_vma=False)
```
